256 devices in a mesh: ctx: 64 (over z, y, core), kv: 4 (over x).
Axes of the slice: x: 4, y: 4, z: 8, core: 2. Of those that a mesh axis runs over, the one named last changes fastest.
Arguments:
- queries: bfloat16 [4, 64, 128], P(None, 'kv'), may hold values from -72 to 72
- keys: bfloat16 [2048, 4, 512, 128], P('ctx', 'kv'), may hold values from -15 to 15
- values: bfloat16 [2048, 4, 512, 128], P('ctx', 'kv'), may hold values from -24 to 24
- lengths: int32 [4], replicated, may hold values from 512 to 262144, as said below
- span_map: int32 [2048], P('ctx'), may hold values from 0 to 2047, each once
- w_out: bfloat16 [8192, 4096], P(None, 'ctx'), may hold values from -0.0625 to 0.0625
Outputs:
- projected: float32 [4, 4096], P(None, 'ctx')
- log_mass: float32 [4, 64], P(None, 'kv')
The draws below stay inside these ranges and needn't reach their ends.
Inputs may be any that keep to these rules, and one draw needn't show every extreme that they name: `lengths`: a multiple of 512; some sequence holds 262144 tokens.
All inputs are finite; a program needn't handle non-finite values.
Results may differ from the reference program's by a relative error of at most 0.003.
Values may be sent and summed in bfloat16 or wider, within the bound.
No kernel may reach another device: no remote copies, remote signals or barrier semaphores. Data moves between devices by JAX's collectives and lax.ppermute only.
A program may use at most 64 MiB of HBM per device.

```python
import math
import jax
import jax.numpy as jnp
from jax import lax

D = 4096
HEADS = 64
KVH = 4
HD = 128
ROWS = 4
SPAN = 512
SPANS = 2048
CPR = 512


def draw_queries(key, part):
    key = jax.random.fold_in(key, 5)
    first = jax.random.fold_in(key, 0)
    base = jax.random.normal(first, (ROWS, HEADS, HD), jnp.float32)
    return jnp.clip(base, -6.0, 6.0).astype(jnp.bfloat16)


def draw_lengths(key, part):
    key = jax.random.fold_in(key, 11)
    first, second = jax.random.split(key)
    counts = jax.random.randint(first, (ROWS,), 1, CPR + 1)
    fullest = jax.random.randint(second, (), 0, ROWS)
    counts = jnp.where(jnp.arange(ROWS) == fullest, CPR, counts)
    return (counts * SPAN).astype(jnp.int32)


def block_levels(key, extent, shards, least, high):
    factor_of, own = 1.0, jax.random.fold_in(key, 6)
    for axis_at, shards_of in shards:
        draws = jnp.exp(jax.random.uniform(jax.random.fold_in(own, axis_at), (shards_of,), jnp.float32, least / len(shards), high / len(shards)))
        factor_of = factor_of * jnp.repeat(draws, extent[axis_at] // shards_of).reshape([-1 if axis == axis_at else 1 for axis in range(len(extent))])
    return factor_of


def normal_values(rng, extent, scale, bound, pieces=(), held_as=jnp.bfloat16):
    entries = jax.random.normal(rng, extent, jnp.float32) * scale
    if len(pieces) > 0:
        entries = block_levels(rng, extent, pieces, -0.22, 0.18) * entries
    return jnp.clip(entries, min=-bound, max=bound).astype(held_as)


def setup_inputs(seed: int = 0) -> dict:
    key_list = jax.random.split(jax.random.key(seed), 7)
    return {
        "queries": draw_queries(jax.random.fold_in(key_list[6], 71), 0),
        "keys": normal_values(key_list[1], (SPANS, KVH, SPAN, HD), 2.5, 15.0, ((0, 64), (1, 4))),
        "values": normal_values(key_list[2], (SPANS, KVH, SPAN, HD), 4.0, 24.0, ((0, 64), (1, 4))),
        "lengths": draw_lengths(jax.random.fold_in(key_list[6], 71), 0),
        "span_map": jax.random.permutation(key_list[4], SPANS).astype(jnp.int32),
        "w_out": normal_values(key_list[5], (HEADS * HD, D), (HEADS * HD) ** -0.5, 0.0625, ((1, 64),)),
    }


def span_terms(query_grouped, keys, values, row_index):
    scale = 1.0 / math.sqrt(HD)

    def one_span(item):
        key_block, value_block, row = item
        query_block = query_grouped[row].astype(jnp.float32)
        scores = jnp.einsum('ghd,gtd->ght', query_block, key_block.astype(jnp.float32)) * scale
        top = lax.optimization_barrier(jnp.max(scores, axis=-1))
        weights = jnp.exp(scores - top[..., None]).astype(jnp.bfloat16)
        total = lax.optimization_barrier(jnp.sum(weights.astype(jnp.float32), axis=-1))
        summed = jnp.einsum('ght,gtd->ghd', weights.astype(jnp.float32), value_block.astype(jnp.float32))
        return (top, total, summed)
    return lax.map(one_span, (keys, values, row_index))

def reference(queries, keys, values, lengths, span_map, w_out):
    query_grouped = queries.reshape(ROWS, KVH, HEADS // KVH, HD)
    row_index = (span_map // CPR).astype(jnp.int32)
    position = span_map % CPR
    live = position * SPAN < lengths[row_index]
    tops, totals, summed = span_terms(query_grouped, keys, values, row_index)
    member = (row_index[:, None] == jnp.arange(ROWS)[None, :]) & live[:, None]
    masked = jnp.where(member[:, :, None, None], tops[:, None], jnp.float32(-1e+30))
    peak = lax.optimization_barrier(jnp.max(masked, axis=0))
    factor = jnp.where(live[:, None, None], jnp.exp(tops - peak[row_index]), jnp.float32(0.0))
    member_f = member.astype(jnp.float32)
    mass = jnp.einsum('cr,cgh->rgh', member_f, factor * totals, precision=lax.Precision.HIGHEST)
    output = jnp.einsum('cr,cghd->rghd', member_f, factor[..., None] * summed, precision=lax.Precision.HIGHEST)
    attended = (output / mass[..., None]).astype(jnp.bfloat16).reshape(ROWS, HEADS * HD)
    log_mass = (peak + jnp.log(mass)).reshape(ROWS, HEADS)
    projected = jnp.dot(attended, w_out, preferred_element_type=jnp.float32)
    return (projected, log_mass)
```

```python
import functools
import math

import jax
import jax.numpy as jnp
from jax import lax
from jax.experimental import pallas as pl
from jax.experimental.pallas import tpu as pltpu
from jax.sharding import Mesh, PartitionSpec as P

ROWS, HD, GROUP, SPAN, CPR = 4, 128, 16, 512, 512
HALF = GROUP // 2
PAIRS = ROWS * HALF
PAY = PAIRS + 8
LANES = 128
BLOCKS = LANES // PAIRS
FLOOR = -1e30
NOTHING = -32000.0
TINY = 2.0**-110
STEPS = 32760.0
SCALE = 1.0 / math.sqrt(HD)
LOG2E = math.log2(math.e)
CHUNK = 4

VMEM = pl.BlockSpec(memory_space=pltpu.VMEM)
SMEM = pl.BlockSpec(memory_space=pltpu.SMEM)
HBM = pl.BlockSpec(memory_space=pltpu.HBM)


def iota(shape, axis):
    return lax.broadcasted_iota(jnp.int32, shape, axis)


def fixed(x):
    return x.astype(jnp.int32).astype(jnp.int16)


def header(lse, power):
    whole = jnp.floor(lse)
    rest = (lse - whole) * 32768.0
    first = jnp.floor(rest)
    second = jnp.floor((rest - first) * 32768.0)
    sub = iota((8, LANES), 0)
    return jnp.where(
        sub == 0,
        whole,
        jnp.where(sub == 1, first, jnp.where(sub == 2, second, jnp.where(sub == 3, power, 0.0))),
    )


def read_headers(in_ref, members):
    tile = in_ref[members[0], PAIRS:PAY].astype(jnp.int32)
    for i in members[1:]:
        tile = tile + in_ref[i, PAIRS:PAY].astype(jnp.int32)
    tile = tile.astype(jnp.float32)
    lse = tile[0:1] + (tile[1:2] * 2.0**-15 + tile[2:3] * 2.0**-30)
    return lse, tile[3:4]


def power_of(out):
    largest = jnp.max(jnp.abs(out), axis=-1, keepdims=True)
    return jnp.ceil(jnp.log2(jnp.maximum(largest, TINY)) * 256.0 + 1.0)


def coded(out, power):
    return jnp.round(out * (jnp.exp2(power * (-1.0 / 256.0)) * STEPS))


def to_row(column, at):
    return jnp.sum(jnp.where(at, column, 0.0), axis=0, keepdims=True)


def stack(in_ref, members):
    return jnp.concatenate(
        [in_ref[i, 0:PAIRS].astype(jnp.int32).astype(jnp.float32) for i in members], axis=0
    )


def over_blocks(x, op):
    step = PAIRS
    while step < LANES:
        x = op(x, pltpu.roll(x, step, 1))
        step *= 2
    return x


def split(x):
    hi = x.astype(jnp.bfloat16)
    return hi, (x - hi.astype(jnp.float32)).astype(jnp.bfloat16)


def split_dot(weights, stacked):
    n = weights.shape[0]
    left = jnp.concatenate(split(weights), axis=0)
    right = jnp.concatenate(split(stacked), axis=1)
    four = jnp.dot(left, right, preferred_element_type=jnp.float32)
    four = four[:n] + four[n:]
    return four[:, :HD] + four[:, HD:]


def attend_kernel(
    q_ref, len_ref, map_ref, k_hbm, v_hbm, out_ref, kbuf, vbuf, qd, m_ref, l_ref, acc_ref, ksem, vsem
):
    slots = kbuf.shape[0]
    chunks = slots // CHUNK

    def copies(i):
        part = pl.ds(i * CHUNK, CHUNK)
        return (
            pltpu.make_async_copy(k_hbm.at[part], kbuf.at[part], ksem.at[i]),
            pltpu.make_async_copy(v_hbm.at[part], vbuf.at[part], vsem.at[i]),
        )

    for i in range(chunks):
        for copy in copies(i):
            copy.start()

    half_span = SPAN // 2
    qd[...] = jnp.zeros_like(qd)
    for r in range(ROWS):
        qd[r, 0:GROUP, 0:HD] = q_ref[r]
        qd[r, GROUP : 2 * GROUP, HD : 2 * HD] = q_ref[r]
    m_ref[...] = jnp.full(m_ref.shape, FLOOR, jnp.float32)
    l_ref[...] = jnp.zeros_like(l_ref)
    acc_ref[...] = jnp.zeros_like(acc_ref)
    exponent = SCALE * LOG2E

    def step(i, carry):
        kcopy, vcopy = copies(i)
        kcopy.wait()
        vcopy.wait()
        for j in range(CHUNK):
            c = i * CHUNK + j
            span = map_ref[c]
            row = lax.shift_right_logical(span, CPR.bit_length() - 1)
            position = lax.bitwise_and(span, CPR - 1)
            live = position * SPAN < len_ref[row]
            keys = jnp.concatenate([kbuf[c, 0:half_span], kbuf[c, half_span:SPAN]], axis=1)
            s = lax.dot_general(
                qd[row], keys, (((1,), (1,)), ((), ())), preferred_element_type=jnp.float32
            )
            top = jnp.max(jnp.maximum(s[:GROUP], s[GROUP:]), axis=1, keepdims=True)
            p = jnp.exp2((s - jnp.concatenate([top, top], axis=0)) * exponent).astype(jnp.bfloat16)
            pf = p.astype(jnp.float32)
            total = jnp.sum(pf[:GROUP] + pf[GROUP:], axis=1, keepdims=True)
            vals = jnp.concatenate([vbuf[c, 0:half_span], vbuf[c, half_span:SPAN]], axis=1)
            o2 = jnp.dot(p, vals, preferred_element_type=jnp.float32)
            o = o2[:GROUP, :HD] + o2[GROUP:, HD:]
            m_old = m_ref[row]
            m_new = jnp.where(live, jnp.maximum(m_old, top), m_old)
            keep = jnp.exp2((m_old - m_new) * exponent)
            add = jnp.where(live, jnp.exp2((top - m_new) * exponent), 0.0)
            m_ref[row] = m_new
            l_ref[row] = keep * l_ref[row] + add * total
            acc_ref[row] = keep * acc_ref[row] + add * o
        return carry

    lax.fori_loop(0, chunks, step, 0)

    l = l_ref[...]
    some = l > 0.0
    safe = jnp.where(some, l, 1.0)
    lse = jnp.where(some, m_ref[...] * SCALE + jnp.log(safe), NOTHING)
    out = acc_ref[...] / safe
    power = power_of(out)
    out = coded(out, power)
    block = lax.rem(lax.axis_index("z") * 2 + lax.axis_index("core"), BLOCKS)
    at = iota((PAIRS, LANES), 1) == iota((PAIRS, LANES), 0) + block * PAIRS
    for c in range(2):
        part = slice(c * HALF, (c + 1) * HALF)
        top = header(
            to_row(lse[:, part].reshape(PAIRS, LANES), at),
            to_row(power[:, part].reshape(PAIRS, 1), at),
        )
        payload = fixed(jnp.concatenate([out[:, part].reshape(PAIRS, HD), top], axis=0))
        for z in range(out_ref.shape[0] // 2):
            out_ref[2 * z + c] = payload


def merge_kernel(in_ref, out_ref):
    groups = in_ref.shape[0] // BLOCKS
    members = [[BLOCKS * j + k for k in range(BLOCKS)] for j in range(groups)]
    heads = [read_headers(in_ref, of) for of in members]
    rows = jnp.concatenate([lse for lse, _ in heads], axis=0)
    powers = jnp.concatenate([power for _, power in heads], axis=0)
    peak = over_blocks(
        jnp.broadcast_to(jnp.max(rows, axis=0, keepdims=True), (8, LANES)), jnp.maximum
    )[0:1]
    weights = jnp.exp(rows - peak)
    mass = over_blocks(
        jnp.broadcast_to(jnp.sum(weights, axis=0, keepdims=True), (8, LANES)), jnp.add
    )[0:1]
    weights = weights * jnp.exp2(powers * (1.0 / 256.0)) / (mass * STEPS)
    lse = peak + jnp.log(mass)
    pair, lane = iota((PAIRS, LANES), 0), iota((PAIRS, LANES), 1)
    spread = jnp.concatenate(
        [jnp.where(lane % PAIRS == pair, weights[j : j + 1], 0.0) for j in range(groups)], axis=1
    )
    out = split_dot(spread, jnp.concatenate([stack(in_ref, of) for of in members], axis=0))
    power = power_of(out)
    block = lax.axis_index("y")
    top = header(
        jnp.where(lane[0:1] // PAIRS == block, lse, 0.0),
        to_row(power, lane == pair + block * PAIRS),
    )
    payload = fixed(jnp.concatenate([coded(out, power), top], axis=0))
    for i in range(out_ref.shape[0]):
        out_ref[i] = payload


def project_kernel(in_ref, w_ref, proj_ref, mass_ref):
    groups = in_ref.shape[0] // BLOCKS
    members = [[groups * k + g for k in range(BLOCKS)] for g in range(groups)]
    heads = [read_headers(in_ref, of) for of in members]
    rows = jnp.concatenate([lse for lse, _ in heads], axis=0)
    powers = jnp.concatenate([power for _, power in heads], axis=0)
    peak = over_blocks(rows, jnp.maximum)
    weights = jnp.exp(rows - peak)
    mass = over_blocks(weights, jnp.add)
    weights = weights * jnp.exp2(powers * (1.0 / 256.0)) / (mass * STEPS)
    lse = peak + jnp.log(mass)
    pair = iota((PAIRS, LANES), 0)
    at = lax.rem(iota((PAIRS, LANES), 1), PAIRS) == lax.rem(pair, ROWS) * HALF + pair // ROWS
    heads = []
    for g in range(groups):
        out = split_dot(jnp.where(at, weights[g : g + 1], 0.0), stack(in_ref, members[g]))
        heads.extend(out[ROWS * h : ROWS * (h + 1)] for h in range(HALF))
    attended = jnp.concatenate(heads, axis=1).astype(jnp.bfloat16)
    proj_ref[...] = lax.dot_general(
        attended, w_ref[...], (((1,), (1,)), ((), ())), preferred_element_type=jnp.float32
    )
    sub, lane = iota((8, LANES), 0), iota((8, LANES), 1)
    result = jnp.zeros((8, LANES), jnp.float32)
    for c in range(2):
        own = jnp.sum(
            jnp.where(sub == lax.axis_index("x") * 2 + c, lse, 0.0), axis=0, keepdims=True
        )
        own = jnp.broadcast_to(own, (8, LANES))
        for r in range(ROWS):
            shifted = pltpu.roll(own, (LANES + c * HALF - r * HALF) % LANES, 1)
            result = jnp.where((sub == r) & (lane // HALF == c), shifted, result)
    mass_ref[...] = result[:ROWS, :GROUP]


def shards(queries, keys, values, lengths, span_map, w_out):
    slots = span_map.shape[0]
    z, y, x = lax.axis_size("z"), lax.axis_size("y"), lax.axis_size("x")
    f32, bf16 = jnp.float32, jnp.bfloat16
    cache = (slots, SPAN, HD)
    part = pl.pallas_call(
        attend_kernel,
        out_shape=jax.ShapeDtypeStruct((z * 2, PAY, HD), jnp.int16),
        in_specs=[VMEM, SMEM, SMEM, HBM, HBM],
        out_specs=VMEM,
        scratch_shapes=[
            pltpu.VMEM(cache, bf16),
            pltpu.VMEM(cache, bf16),
            pltpu.VMEM((ROWS, 2 * GROUP, 2 * HD), bf16),
            pltpu.VMEM((ROWS, GROUP, LANES), f32),
            pltpu.VMEM((ROWS, GROUP, LANES), f32),
            pltpu.VMEM((ROWS, GROUP, HD), f32),
            pltpu.SemaphoreType.DMA((slots // CHUNK,)),
            pltpu.SemaphoreType.DMA((slots // CHUNK,)),
        ],
        compiler_params=pltpu.CompilerParams(vmem_limit_bytes=60 * 2**20),
        name="attend",
    )(queries, lengths, span_map, keys.reshape(cache), values.reshape(cache))
    part = lax.all_to_all(part, ("z", "core"), 0, 0, tiled=True)
    part = pl.pallas_call(
        merge_kernel,
        out_shape=jax.ShapeDtypeStruct((y * x * 2, PAY, HD), jnp.int16),
        in_specs=[VMEM],
        out_specs=VMEM,
        compiler_params=pltpu.CompilerParams(vmem_limit_bytes=8 * 2**20),
        name="merge",
    )(part)
    part = lax.all_to_all(part, ("y", "x", "core"), 0, 0, tiled=True)
    return pl.pallas_call(
        project_kernel,
        out_shape=(
            jax.ShapeDtypeStruct((ROWS, w_out.shape[1]), f32),
            jax.ShapeDtypeStruct((ROWS, GROUP), f32),
        ),
        in_specs=[VMEM, VMEM],
        out_specs=(VMEM, VMEM),
        compiler_params=pltpu.CompilerParams(vmem_limit_bytes=8 * 2**20),
        name="project",
    )(part, w_out.T)


def solution(mesh):
    fine = Mesh(mesh.devices.reshape(8, 4, 2, 4), ("z", "y", "core", "x"))
    ctx = ("z", "y", "core")
    placed = (
        P(None, "x", None),
        P(ctx, "x", None, None),
        P(ctx, "x", None, None),
        P(),
        P(ctx),
        P(None, ctx),
    )
    return jax.shard_map(
        shards,
        mesh=fine,
        in_specs=placed,
        out_specs=(P(None, ctx), P(None, "x")),
        check_vma=False,
    )
```

```python
import functools
import math

import jax
import jax.numpy as jnp
from jax import lax
from jax.experimental import pallas as pl
from jax.experimental.pallas import tpu as pltpu
from jax.sharding import Mesh, PartitionSpec as P

ROWS, HD, GROUP, SPAN, CPR = 4, 128, 16, 512, 512
HALF = GROUP // 2
PAIRS = ROWS * HALF
PAY = PAIRS + 8
LANES = 128
BLOCKS = LANES // PAIRS
FLOOR = -1e30
NOTHING = -32000.0
TINY = 2.0**-110
STEPS = 32760.0
SCALE = 1.0 / math.sqrt(HD)
LOG2E = math.log2(math.e)
CHUNKS = 2

VMEM = pl.BlockSpec(memory_space=pltpu.VMEM)
HBM = pl.BlockSpec(memory_space=pltpu.HBM)


def iota(shape, axis):
    return lax.broadcasted_iota(jnp.int32, shape, axis)


def fixed(x):
    return x.astype(jnp.int32).astype(jnp.int16)


def header(lse, power):
    whole = jnp.floor(lse)
    rest = (lse - whole) * 32768.0
    first = jnp.floor(rest)
    second = jnp.floor((rest - first) * 32768.0)
    sub = iota((8, LANES), 0)
    return jnp.where(
        sub == 0,
        whole,
        jnp.where(sub == 1, first, jnp.where(sub == 2, second, jnp.where(sub == 3, power, 0.0))),
    )


def read_headers(in_ref, members):
    tile = in_ref[members[0], PAIRS:PAY].astype(jnp.int32)
    for i in members[1:]:
        tile = tile + in_ref[i, PAIRS:PAY].astype(jnp.int32)
    tile = tile.astype(jnp.float32)
    lse = tile[0:1] + (tile[1:2] * 2.0**-15 + tile[2:3] * 2.0**-30)
    return lse, tile[3:4]


def power_of(out):
    largest = jnp.max(jnp.abs(out), axis=-1, keepdims=True)
    return jnp.ceil(jnp.log2(jnp.maximum(largest, TINY)) * 256.0 + 1.0)


def coded(out, power):
    return jnp.round(out * (jnp.exp2(power * (-1.0 / 256.0)) * STEPS))


def to_row(column, at):
    return jnp.sum(jnp.where(at, column, 0.0), axis=0, keepdims=True)


def stack(in_ref, members):
    return jnp.concatenate(
        [in_ref[i, 0:PAIRS].astype(jnp.int32).astype(jnp.float32) for i in members], axis=0
    )


def over_blocks(x, op):
    step = PAIRS
    while step < LANES:
        x = op(x, pltpu.roll(x, step, 1))
        step *= 2
    return x


def split(x):
    hi = x.astype(jnp.bfloat16)
    return hi, (x - hi.astype(jnp.float32)).astype(jnp.bfloat16)


def split_dot(weights, stacked):
    n = weights.shape[0]
    left = jnp.concatenate(split(weights), axis=0)
    right = jnp.concatenate(split(stacked), axis=1)
    four = jnp.dot(left, right, preferred_element_type=jnp.float32)
    four = four[:n] + four[n:]
    return four[:, :HD] + four[:, HD:]


def attend_kernel(
    q_hbm, len_hbm, map_hbm, k_hbm, v_hbm, out_ref,
    q_ref, len_ref, map_ref, kbuf, vbuf, s_ref, m_ref, l_ref, acc_ref, sem, ksem, vsem,
):
    slots = kbuf.shape[0]
    size = slots // CHUNKS
    parts = [pl.ds(i * size, size) for i in range(CHUNKS)]
    small = [
        pltpu.make_async_copy(source, target, sem.at[i])
        for i, (source, target) in enumerate(
            [(map_hbm, map_ref), (len_hbm, len_ref), (q_hbm, q_ref)]
        )
    ]
    kcopies = [
        pltpu.make_async_copy(k_hbm.at[part], kbuf.at[part], ksem.at[i])
        for i, part in enumerate(parts)
    ]
    vcopies = [
        pltpu.make_async_copy(v_hbm.at[part], vbuf.at[part], vsem.at[i])
        for i, part in enumerate(parts)
    ]
    for copy in small + kcopies:
        copy.start(priority=0)
    for copy in vcopies:
        copy.start(priority=1)
    m_ref[...] = jnp.full(m_ref.shape, FLOOR, jnp.float32)
    l_ref[...] = jnp.zeros_like(l_ref)
    acc_ref[...] = jnp.zeros_like(acc_ref)
    for copy in small:
        copy.wait()

    def place(c):
        span = map_ref[c]
        row = lax.shift_right_logical(span, CPR.bit_length() - 1)
        return row, lax.bitwise_and(span, CPR - 1) * SPAN < len_ref[row]

    def folded(x, op):
        tiles = [x[:, i * LANES : (i + 1) * LANES] for i in range(SPAN // LANES)]
        return op(op(tiles[0], tiles[1]), op(tiles[2], tiles[3]))

    for i, copy in enumerate(kcopies):
        copy.wait()
        for c in range(i * size, (i + 1) * size):
            row, live = place(c)
            s = lax.dot_general(
                q_ref[row], kbuf[c], (((1,), (1,)), ((), ())), preferred_element_type=jnp.float32
            )
            s_ref[c] = s
            m_ref[row] = jnp.maximum(
                m_ref[row], jnp.where(live, folded(s, jnp.maximum), FLOOR)
            )
    m_ref[...] = jnp.broadcast_to(jnp.max(m_ref[...], axis=2, keepdims=True), m_ref.shape)

    for i, copy in enumerate(vcopies):
        copy.wait()
        for c in range(i * size, (i + 1) * size):
            row, live = place(c)
            top = jnp.where(live, m_ref[row], -FLOOR)
            top = jnp.concatenate([top] * (SPAN // LANES), axis=1)
            p = jnp.exp2((s_ref[c] - top) * (SCALE * LOG2E)).astype(jnp.bfloat16)
            l_ref[row] += folded(p.astype(jnp.float32), jnp.add)
            acc_ref[row] += jnp.dot(p, vbuf[c], preferred_element_type=jnp.float32)

    l = jnp.broadcast_to(jnp.sum(l_ref[...], axis=2, keepdims=True), l_ref.shape)
    some = l > 0.0
    safe = jnp.where(some, l, 1.0)
    lse = jnp.where(some, m_ref[...] * SCALE + jnp.log(safe), NOTHING)
    out = acc_ref[...] / safe
    power = power_of(out)
    out = coded(out, power)
    block = lax.rem(lax.axis_index("z") * 2 + lax.axis_index("core"), BLOCKS)
    at = iota((PAIRS, LANES), 1) == iota((PAIRS, LANES), 0) + block * PAIRS
    for c in range(2):
        part = slice(c * HALF, (c + 1) * HALF)
        top = header(
            to_row(lse[:, part].reshape(PAIRS, LANES), at),
            to_row(power[:, part].reshape(PAIRS, 1), at),
        )
        payload = fixed(jnp.concatenate([out[:, part].reshape(PAIRS, HD), top], axis=0))
        for z in range(out_ref.shape[0] // 2):
            out_ref[2 * z + c] = payload


def merge_kernel(in_ref, out_ref):
    groups = in_ref.shape[0] // BLOCKS
    members = [[BLOCKS * j + k for k in range(BLOCKS)] for j in range(groups)]
    heads = [read_headers(in_ref, of) for of in members]
    rows = jnp.concatenate([lse for lse, _ in heads], axis=0)
    powers = jnp.concatenate([power for _, power in heads], axis=0)
    peak = over_blocks(
        jnp.broadcast_to(jnp.max(rows, axis=0, keepdims=True), (8, LANES)), jnp.maximum
    )[0:1]
    weights = jnp.exp(rows - peak)
    mass = over_blocks(
        jnp.broadcast_to(jnp.sum(weights, axis=0, keepdims=True), (8, LANES)), jnp.add
    )[0:1]
    weights = weights * jnp.exp2(powers * (1.0 / 256.0)) / (mass * STEPS)
    lse = peak + jnp.log(mass)
    pair, lane = iota((PAIRS, LANES), 0), iota((PAIRS, LANES), 1)
    spread = jnp.concatenate(
        [jnp.where(lane % PAIRS == pair, weights[j : j + 1], 0.0) for j in range(groups)], axis=1
    )
    out = split_dot(spread, jnp.concatenate([stack(in_ref, of) for of in members], axis=0))
    power = power_of(out)
    block = lax.axis_index("y")
    top = header(
        jnp.where(lane[0:1] // PAIRS == block, lse, 0.0),
        to_row(power, lane == pair + block * PAIRS),
    )
    payload = fixed(jnp.concatenate([coded(out, power), top], axis=0))
    for i in range(out_ref.shape[0]):
        out_ref[i] = payload


def project_kernel(in_ref, w_ref, proj_ref, mass_ref):
    groups = in_ref.shape[0] // BLOCKS
    members = [[groups * k + g for k in range(BLOCKS)] for g in range(groups)]
    heads = [read_headers(in_ref, of) for of in members]
    rows = jnp.concatenate([lse for lse, _ in heads], axis=0)
    powers = jnp.concatenate([power for _, power in heads], axis=0)
    peak = over_blocks(rows, jnp.maximum)
    weights = jnp.exp(rows - peak)
    mass = over_blocks(weights, jnp.add)
    weights = weights * jnp.exp2(powers * (1.0 / 256.0)) / (mass * STEPS)
    lse = peak + jnp.log(mass)
    pair = iota((PAIRS, LANES), 0)
    at = lax.rem(iota((PAIRS, LANES), 1), PAIRS) == lax.rem(pair, ROWS) * HALF + pair // ROWS
    heads = []
    for g in range(groups):
        out = split_dot(jnp.where(at, weights[g : g + 1], 0.0), stack(in_ref, members[g]))
        heads.extend(out[ROWS * h : ROWS * (h + 1)] for h in range(HALF))
    attended = jnp.concatenate(heads, axis=1).astype(jnp.bfloat16)
    proj_ref[...] = lax.dot_general(
        attended, w_ref[...], (((1,), (1,)), ((), ())), preferred_element_type=jnp.float32
    )
    sub, lane = iota((8, LANES), 0), iota((8, LANES), 1)
    result = jnp.zeros((8, LANES), jnp.float32)
    for c in range(2):
        own = jnp.sum(
            jnp.where(sub == lax.axis_index("x") * 2 + c, lse, 0.0), axis=0, keepdims=True
        )
        own = jnp.broadcast_to(own, (8, LANES))
        for r in range(ROWS):
            shifted = pltpu.roll(own, (LANES + c * HALF - r * HALF) % LANES, 1)
            result = jnp.where((sub == r) & (lane // HALF == c), shifted, result)
    mass_ref[...] = result[:ROWS, :GROUP]


def shards(queries, keys, values, lengths, span_map, w_out):
    slots = span_map.shape[0]
    z, y, x = lax.axis_size("z"), lax.axis_size("y"), lax.axis_size("x")
    f32, bf16 = jnp.float32, jnp.bfloat16
    cache = (slots, SPAN, HD)
    part = pl.pallas_call(
        attend_kernel,
        out_shape=jax.ShapeDtypeStruct((z * 2, PAY, HD), jnp.int16),
        in_specs=[HBM] * 5,
        out_specs=VMEM,
        scratch_shapes=[
            pltpu.VMEM((ROWS, GROUP, HD), bf16),
            pltpu.SMEM((ROWS,), jnp.int32),
            pltpu.SMEM((slots,), jnp.int32),
            pltpu.VMEM(cache, bf16),
            pltpu.VMEM(cache, bf16),
            pltpu.VMEM((slots, GROUP, SPAN), f32),
            pltpu.VMEM((ROWS, GROUP, LANES), f32),
            pltpu.VMEM((ROWS, GROUP, LANES), f32),
            pltpu.VMEM((ROWS, GROUP, HD), f32),
            pltpu.SemaphoreType.DMA((3,)),
            pltpu.SemaphoreType.DMA((CHUNKS,)),
            pltpu.SemaphoreType.DMA((CHUNKS,)),
        ],
        compiler_params=pltpu.CompilerParams(vmem_limit_bytes=60 * 2**20),
        name="attend",
    )(queries, lengths, span_map, keys.reshape(cache), values.reshape(cache))
    part = lax.all_to_all(part, ("z", "core"), 0, 0, tiled=True)
    part = pl.pallas_call(
        merge_kernel,
        out_shape=jax.ShapeDtypeStruct((y * x * 2, PAY, HD), jnp.int16),
        in_specs=[VMEM],
        out_specs=VMEM,
        compiler_params=pltpu.CompilerParams(vmem_limit_bytes=8 * 2**20),
        name="merge",
    )(part)
    part = lax.all_to_all(part, ("y", "x", "core"), 0, 0, tiled=True)
    return pl.pallas_call(
        project_kernel,
        out_shape=(
            jax.ShapeDtypeStruct((ROWS, w_out.shape[1]), f32),
            jax.ShapeDtypeStruct((ROWS, GROUP), f32),
        ),
        in_specs=[VMEM, VMEM],
        out_specs=(VMEM, VMEM),
        compiler_params=pltpu.CompilerParams(vmem_limit_bytes=8 * 2**20),
        name="project",
    )(part, w_out.T)


def solution(mesh):
    fine = Mesh(mesh.devices.reshape(8, 4, 2, 4), ("z", "y", "core", "x"))
    ctx = ("z", "y", "core")
    placed = (
        P(None, "x", None),
        P(ctx, "x", None, None),
        P(ctx, "x", None, None),
        P(),
        P(ctx),
        P(None, ctx),
    )
    return jax.shard_map(
        shards,
        mesh=fine,
        in_specs=placed,
        out_specs=(P(None, ctx), P(None, "x")),
        check_vma=False,
    )
```

```python
import functools
import math

import jax
import jax.numpy as jnp
from jax import lax
from jax.experimental import pallas as pl
from jax.experimental.pallas import tpu as pltpu
from jax.sharding import Mesh, PartitionSpec as P

ROWS, HD, GROUP, SPAN, CPR = 4, 128, 16, 512, 512
HALF = GROUP // 2
PAIRS = ROWS * HALF
PAY = PAIRS + 2
LANES = 128
BLOCKS = LANES // PAIRS
FLOOR = -1e30
NOTHING = -32000.0
TINY = 2.0**-110
STEPS = 32760.0
SCALE = 1.0 / math.sqrt(HD)
LOG2E = math.log2(math.e)
CHUNKS = 2

VMEM = pl.BlockSpec(memory_space=pltpu.VMEM)
HBM = pl.BlockSpec(memory_space=pltpu.HBM)


def iota(shape, axis):
    return lax.broadcasted_iota(jnp.int32, shape, axis)


def fixed(x):
    return x.astype(jnp.int32).astype(jnp.int16)


def header(lse, power):
    whole = jnp.floor(lse)
    rest = (lse - whole) * 32768.0
    first = jnp.floor(rest)
    second = jnp.floor((rest - first) * 32768.0)
    shape = (PAIRS, LANES)
    block = iota(shape, 1) // PAIRS
    kind = jnp.where(block == 0, whole, jnp.where(block == 1, first, second))
    kind = jnp.where(block == 3, power, kind)
    row = jnp.sum(
        jnp.where(iota(shape, 1) % PAIRS == iota(shape, 0), kind, 0.0), axis=0, keepdims=True
    )
    return jnp.broadcast_to(row, (2, LANES))


def read_headers(flat, members):
    rows = [flat[i, PAIRS:PAY].astype(jnp.int32).astype(jnp.float32)[0:1] for i in members]
    rows = jnp.concatenate(rows, axis=0)
    block = iota(rows.shape, 1) // PAIRS
    unit = jnp.where(block == 0, 1.0, jnp.where(block == 1, 2.0**-15, 2.0**-30))
    lse = over_blocks(jnp.where(block == 3, 0.0, rows * unit), jnp.add)
    scale = over_blocks(jnp.where(block == 3, rows, 0.0), jnp.add)
    return lse, jnp.exp2(scale * (1.0 / 256.0)) * (1.0 / STEPS)


def by_block(tiles):
    block = iota(tiles[0].shape, 1) // PAIRS
    out = tiles[0]
    for k in range(1, BLOCKS):
        out = jnp.where(block == k, tiles[k], out)
    return out


def power_of(out):
    largest = jnp.max(jnp.abs(out), axis=-1, keepdims=True)
    return jnp.ceil(jnp.log2(jnp.maximum(largest, TINY)) * 256.0 + 1.0)


def coded(out, power):
    return jnp.round(out * (jnp.exp2(power * (-1.0 / 256.0)) * STEPS))


def stack(flat, members):
    return jnp.concatenate(
        [flat[i, 0:PAIRS].astype(jnp.int32).astype(jnp.float32) for i in members], axis=0
    )


def over_blocks(x, op):
    step = PAIRS
    while step < LANES:
        x = op(x, pltpu.roll(x, step, 1))
        step *= 2
    return x


def split(x):
    hi = x.astype(jnp.bfloat16)
    return hi, (x - hi.astype(jnp.float32)).astype(jnp.bfloat16)


def split_dot(weights, stacked):
    n = weights.shape[0]
    left = jnp.concatenate(split(weights), axis=0)
    right = jnp.concatenate(split(stacked), axis=1)
    four = jnp.dot(left, right, preferred_element_type=jnp.float32)
    four = four[:n] + four[n:]
    return four[:, :HD] + four[:, HD:]


def attend_kernel(
    q_hbm, len_hbm, map_hbm, k_hbm, v_hbm, out_ref,
    q_ref, len_ref, map_ref, kbuf, vbuf, s_ref, m_ref, l_ref, acc_ref, sem, ksem, vsem,
):
    slots = kbuf.shape[0]
    size = slots // CHUNKS
    parts = [pl.ds(i * size, size) for i in range(CHUNKS)]
    small = [
        pltpu.make_async_copy(source, target, sem.at[i])
        for i, (source, target) in enumerate(
            [(map_hbm, map_ref), (len_hbm, len_ref), (q_hbm, q_ref)]
        )
    ]
    kcopies = [
        pltpu.make_async_copy(k_hbm.at[part], kbuf.at[part], ksem.at[i])
        for i, part in enumerate(parts)
    ]
    vcopies = [
        pltpu.make_async_copy(v_hbm.at[part], vbuf.at[part], vsem.at[i])
        for i, part in enumerate(parts)
    ]
    for copy in small + kcopies:
        copy.start(priority=0)
    for copy in vcopies:
        copy.start(priority=1)
    m_ref[...] = jnp.full(m_ref.shape, FLOOR, jnp.float32)
    l_ref[...] = jnp.zeros_like(l_ref)
    acc_ref[...] = jnp.zeros_like(acc_ref)
    for copy in small:
        copy.wait()

    def place(c):
        span = map_ref[c]
        row = lax.shift_right_logical(span, CPR.bit_length() - 1)
        return row, lax.bitwise_and(span, CPR - 1) * SPAN < len_ref[row]

    def folded(x, op):
        tiles = [x[:, i * LANES : (i + 1) * LANES] for i in range(SPAN // LANES)]
        return op(op(tiles[0], tiles[1]), op(tiles[2], tiles[3]))

    for i, copy in enumerate(kcopies):
        copy.wait()
        for c in range(i * size, (i + 1) * size):
            row, live = place(c)
            s = lax.dot_general(
                q_ref[row], kbuf[c], (((1,), (1,)), ((), ())), preferred_element_type=jnp.float32
            )
            s_ref[c] = s
            m_ref[row] = jnp.maximum(
                m_ref[row], jnp.where(live, folded(s, jnp.maximum), FLOOR)
            )
    m_ref[...] = jnp.broadcast_to(jnp.max(m_ref[...], axis=2, keepdims=True), m_ref.shape)

    for i, copy in enumerate(vcopies):
        copy.wait()
        for c in range(i * size, (i + 1) * size):
            row, live = place(c)
            top = jnp.where(live, m_ref[row], -FLOOR)
            top = jnp.concatenate([top] * (SPAN // LANES), axis=1)
            p = jnp.exp2((s_ref[c] - top) * (SCALE * LOG2E)).astype(jnp.bfloat16)
            l_ref[row] += folded(p.astype(jnp.float32), jnp.add)
            acc_ref[row] += jnp.dot(p, vbuf[c], preferred_element_type=jnp.float32)

    l = jnp.broadcast_to(jnp.sum(l_ref[...], axis=2, keepdims=True), l_ref.shape)
    some = l > 0.0
    safe = jnp.where(some, l, 1.0)
    lse = jnp.where(some, m_ref[...] * SCALE + jnp.log(safe), NOTHING)
    out = acc_ref[...] / safe
    power = power_of(out)
    out = coded(out, power)
    flat = out_ref.reshape(out_ref.shape[0], PAY, HD)
    for c in range(2):
        part = slice(c * HALF, (c + 1) * HALF)
        top = header(lse[:, part].reshape(PAIRS, LANES), power[:, part].reshape(PAIRS, 1))
        payload = fixed(jnp.concatenate([out[:, part].reshape(PAIRS, HD), top], axis=0))
        for z in range(out_ref.shape[0] // 2):
            flat[2 * z + c] = payload


def merge_kernel(in_ref, out_ref):
    flat = in_ref.reshape(in_ref.shape[0], PAY, HD)
    halves = [range(0, 8), range(8, 16)]
    heads = [read_headers(flat, half) for half in halves]
    peak = jnp.max(jnp.maximum(heads[0][0], heads[1][0]), axis=0, keepdims=True)
    weights = [jnp.exp(lse - peak) for lse, _ in heads]
    mass = jnp.sum(weights[0] + weights[1], axis=0, keepdims=True)
    lse = peak + jnp.log(mass)
    weights = [w * scale / mass for w, (_, scale) in zip(weights, heads)]
    groups = BLOCKS
    rows = by_block([t for w in weights for t in (w, pltpu.roll(w, 4, 0))])
    at = iota((PAIRS, LANES), 1) % PAIRS == iota((PAIRS, LANES), 0)
    spread = jnp.concatenate(
        [jnp.where(at, rows[g : g + 1], 0.0) for g in range(groups)], axis=1
    )
    members = [k * groups + g for g in range(groups) for k in range(BLOCKS)]
    out = split_dot(spread, stack(flat, members))
    power = power_of(out)
    payload = fixed(jnp.concatenate([coded(out, power), header(lse, power)], axis=0))
    sent = out_ref.reshape(out_ref.shape[0], PAY, HD)
    for i in range(out_ref.shape[0]):
        sent[i] = payload


def project_kernel(in_ref, w_ref, proj_ref, mass_ref):
    flat = in_ref.reshape(in_ref.shape[0], PAY, HD)
    groups = in_ref.shape[0] // BLOCKS
    heads = [read_headers(flat, range(groups * y, groups * (y + 1))) for y in range(BLOCKS)]
    peak = functools.reduce(jnp.maximum, [lse for lse, _ in heads])
    weights = [jnp.exp(lse - peak) for lse, _ in heads]
    mass = functools.reduce(jnp.add, weights)
    lse = peak + jnp.log(mass)
    weights = by_block([w * scale / mass for w, (_, scale) in zip(weights, heads)])
    pair = iota((PAIRS, LANES), 0)
    at = lax.rem(iota((PAIRS, LANES), 1), PAIRS) == lax.rem(pair, ROWS) * HALF + pair // ROWS
    heads = []
    for g in range(groups):
        out = split_dot(jnp.where(at, weights[g : g + 1], 0.0), stack(flat, [groups * y + g for y in range(BLOCKS)]))
        heads.extend(out[ROWS * h : ROWS * (h + 1)] for h in range(HALF))
    attended = jnp.concatenate(heads, axis=1).astype(jnp.bfloat16)
    proj_ref[...] = lax.dot_general(
        attended, w_ref[...], (((1,), (1,)), ((), ())), preferred_element_type=jnp.float32
    )
    sub, lane = iota((8, LANES), 0), iota((8, LANES), 1)
    result = jnp.zeros((8, LANES), jnp.float32)
    for c in range(2):
        own = jnp.sum(
            jnp.where(sub == lax.axis_index("x") * 2 + c, lse, 0.0), axis=0, keepdims=True
        )
        own = jnp.broadcast_to(own, (8, LANES))
        for r in range(ROWS):
            shifted = pltpu.roll(own, (LANES + c * HALF - r * HALF) % LANES, 1)
            result = jnp.where((sub == r) & (lane // HALF == c), shifted, result)
    mass_ref[...] = result[:ROWS, :GROUP]


def shards(queries, keys, values, lengths, span_map, w_out):
    slots = span_map.shape[0]
    z, y, x = lax.axis_size("z"), lax.axis_size("y"), lax.axis_size("x")
    f32, bf16 = jnp.float32, jnp.bfloat16
    cache = (slots, SPAN, HD)
    part = pl.pallas_call(
        attend_kernel,
        out_shape=jax.ShapeDtypeStruct((z * 2, PAY // 2, 2, HD), jnp.int16),
        in_specs=[HBM] * 5,
        out_specs=VMEM,
        scratch_shapes=[
            pltpu.VMEM((ROWS, GROUP, HD), bf16),
            pltpu.SMEM((ROWS,), jnp.int32),
            pltpu.SMEM((slots,), jnp.int32),
            pltpu.VMEM(cache, bf16),
            pltpu.VMEM(cache, bf16),
            pltpu.VMEM((slots, GROUP, SPAN), f32),
            pltpu.VMEM((ROWS, GROUP, LANES), f32),
            pltpu.VMEM((ROWS, GROUP, LANES), f32),
            pltpu.VMEM((ROWS, GROUP, HD), f32),
            pltpu.SemaphoreType.DMA((3,)),
            pltpu.SemaphoreType.DMA((CHUNKS,)),
            pltpu.SemaphoreType.DMA((CHUNKS,)),
        ],
        compiler_params=pltpu.CompilerParams(vmem_limit_bytes=60 * 2**20),
        name="attend",
    )(queries, lengths, span_map, keys.reshape(cache), values.reshape(cache))
    part = lax.all_to_all(part, ("z", "core"), 0, 0, tiled=True)
    part = pl.pallas_call(
        merge_kernel,
        out_shape=jax.ShapeDtypeStruct((y * x * 2, PAY // 2, 2, HD), jnp.int16),
        in_specs=[VMEM],
        out_specs=VMEM,
        compiler_params=pltpu.CompilerParams(vmem_limit_bytes=8 * 2**20),
        name="merge",
    )(part)
    part = lax.all_to_all(part, ("y", "x", "core"), 0, 0, tiled=True)
    return pl.pallas_call(
        project_kernel,
        out_shape=(
            jax.ShapeDtypeStruct((ROWS, w_out.shape[1]), f32),
            jax.ShapeDtypeStruct((ROWS, GROUP), f32),
        ),
        in_specs=[VMEM, VMEM],
        out_specs=(VMEM, VMEM),
        compiler_params=pltpu.CompilerParams(vmem_limit_bytes=8 * 2**20),
        name="project",
    )(part, w_out.T)


def solution(mesh):
    fine = Mesh(mesh.devices.reshape(8, 4, 2, 4), ("z", "y", "core", "x"))
    ctx = ("z", "y", "core")
    placed = (
        P(None, "x", None),
        P(ctx, "x", None, None),
        P(ctx, "x", None, None),
        P(),
        P(ctx),
        P(None, ctx),
    )
    return jax.shard_map(
        shards,
        mesh=fine,
        in_specs=placed,
        out_specs=(P(None, ctx), P(None, "x")),
        check_vma=False,
    )
```

```python
import functools
import math

import jax
import jax.numpy as jnp
from jax import lax
from jax.experimental import pallas as pl
from jax.experimental.pallas import tpu as pltpu
from jax.sharding import Mesh, PartitionSpec as P

ROWS, HD, GROUP, SPAN, CPR = 4, 128, 16, 512, 512
HALF = GROUP // 2
PAIRS = ROWS * HALF
PAY = PAIRS + 2
LANES = 128
BLOCKS = LANES // PAIRS
FLOOR = -1e30
NOTHING = -32000.0
TINY = 2.0**-110
STEPS = 32760.0
SCALE = 1.0 / math.sqrt(HD)
LOG2E = math.log2(math.e)
KEY_PARTS = (16, 16)
VALUE_PARTS = (16, 16)

VMEM = pl.BlockSpec(memory_space=pltpu.VMEM)
HBM = pl.BlockSpec(memory_space=pltpu.HBM)


def iota(shape, axis):
    return lax.broadcasted_iota(jnp.int32, shape, axis)


def fixed(x):
    return x.astype(jnp.int32).astype(jnp.int16)


def header(lse, power):
    whole = jnp.floor(lse)
    rest = (lse - whole) * 32768.0
    first = jnp.floor(rest)
    second = jnp.floor((rest - first) * 32768.0)
    shape = (PAIRS, LANES)
    block = iota(shape, 1) // PAIRS
    kind = jnp.where(block == 0, whole, jnp.where(block == 1, first, second))
    kind = jnp.where(block == 3, power, kind)
    row = jnp.sum(
        jnp.where(iota(shape, 1) % PAIRS == iota(shape, 0), kind, 0.0), axis=0, keepdims=True
    )
    return jnp.broadcast_to(row, (2, LANES))


def read_headers(flat, members):
    rows = [flat[i, PAIRS:PAY].astype(jnp.int32).astype(jnp.float32)[0:1] for i in members]
    rows = jnp.concatenate(rows, axis=0)
    block = iota(rows.shape, 1) // PAIRS
    unit = jnp.where(block == 0, 1.0, jnp.where(block == 1, 2.0**-15, 2.0**-30))
    lse = over_blocks(jnp.where(block == 3, 0.0, rows * unit), jnp.add)
    scale = over_blocks(jnp.where(block == 3, rows, 0.0), jnp.add)
    return lse, jnp.exp2(scale * (1.0 / 256.0)) * (1.0 / STEPS)


def by_block(tiles):
    block = iota(tiles[0].shape, 1) // PAIRS
    out = tiles[0]
    for k in range(1, BLOCKS):
        out = jnp.where(block == k, tiles[k], out)
    return out


def power_of(out):
    largest = jnp.max(jnp.abs(out), axis=-1, keepdims=True)
    return jnp.ceil(jnp.log2(jnp.maximum(largest, TINY)) * 256.0 + 1.0)


def coded(out, power):
    return jnp.round(out * (jnp.exp2(power * (-1.0 / 256.0)) * STEPS))


def stack(flat, members):
    return jnp.concatenate(
        [flat[i, 0:PAIRS].astype(jnp.int32).astype(jnp.float32) for i in members], axis=0
    )


def over_blocks(x, op):
    step = PAIRS
    while step < LANES:
        x = op(x, pltpu.roll(x, step, 1))
        step *= 2
    return x


def split(x):
    hi = x.astype(jnp.bfloat16)
    return hi, (x - hi.astype(jnp.float32)).astype(jnp.bfloat16)


def split_dot(weights, stacked):
    n = weights.shape[0]
    left = jnp.concatenate(split(weights), axis=0)
    right = jnp.concatenate(split(stacked), axis=1)
    four = jnp.dot(left, right, preferred_element_type=jnp.float32)
    four = four[:n] + four[n:]
    return four[:, :HD] + four[:, HD:]


def attend_kernel(
    q_hbm, len_hbm, map_hbm, k_hbm, v_hbm, out_ref,
    q_ref, len_ref, map_ref, kbuf, vbuf, s_ref, m_ref, l_ref, acc_ref, sem, ksem, vsem,
):
    small = [
        pltpu.make_async_copy(source, target, sem.at[i])
        for i, (source, target) in enumerate(
            [(map_hbm, map_ref), (len_hbm, len_ref), (q_hbm, q_ref)]
        )
    ]

    def copies(source, target, sems, sizes):
        at = [sum(sizes[:i]) for i in range(len(sizes))]
        return [range(start, start + size) for start, size in zip(at, sizes)], [
            pltpu.make_async_copy(
                source.at[pl.ds(start, size)], target.at[pl.ds(start, size)], sems.at[i]
            )
            for i, (start, size) in enumerate(zip(at, sizes))
        ]

    kparts, kcopies = copies(k_hbm, kbuf, ksem, KEY_PARTS)
    vparts, vcopies = copies(v_hbm, vbuf, vsem, VALUE_PARTS)
    for copy in small + kcopies:
        copy.start(priority=0)
    for copy in vcopies:
        copy.start(priority=1)
    m_ref[...] = jnp.full(m_ref.shape, FLOOR, jnp.float32)
    l_ref[...] = jnp.zeros_like(l_ref)
    acc_ref[...] = jnp.zeros_like(acc_ref)
    for copy in small:
        copy.wait()

    def place(c):
        span = map_ref[c]
        row = lax.shift_right_logical(span, CPR.bit_length() - 1)
        return row, lax.bitwise_and(span, CPR - 1) * SPAN < len_ref[row]

    def folded(x, op):
        tiles = [x[:, i * LANES : (i + 1) * LANES] for i in range(SPAN // LANES)]
        return op(op(tiles[0], tiles[1]), op(tiles[2], tiles[3]))

    for part, copy in zip(kparts, kcopies):
        copy.wait()
        for c in part:
            row, live = place(c)
            s = lax.dot_general(
                q_ref[row], kbuf[c], (((1,), (1,)), ((), ())), preferred_element_type=jnp.float32
            )
            s_ref[c] = s
            m_ref[row] = jnp.maximum(
                m_ref[row], jnp.where(live, folded(s, jnp.maximum), FLOOR)
            )
    m_ref[...] = jnp.broadcast_to(jnp.max(m_ref[...], axis=2, keepdims=True), m_ref.shape)

    for part, copy in zip(vparts, vcopies):
        copy.wait()
        for c in part:
            row, live = place(c)
            top = jnp.where(live, m_ref[row], -FLOOR)
            top = jnp.concatenate([top] * (SPAN // LANES), axis=1)
            p = jnp.exp2((s_ref[c] - top) * (SCALE * LOG2E)).astype(jnp.bfloat16)
            l_ref[row] += folded(p.astype(jnp.float32), jnp.add)
            acc_ref[row] += jnp.dot(p, vbuf[c], preferred_element_type=jnp.float32)

    l = jnp.broadcast_to(jnp.sum(l_ref[...], axis=2, keepdims=True), l_ref.shape)
    some = l > 0.0
    safe = jnp.where(some, l, 1.0)
    lse = jnp.where(some, m_ref[...] * SCALE + jnp.log(safe), NOTHING)
    out = acc_ref[...] / safe
    power = power_of(out)
    out = coded(out, power)
    flat = out_ref.reshape(out_ref.shape[0], PAY, HD)
    for c in range(2):
        part = slice(c * HALF, (c + 1) * HALF)
        top = header(lse[:, part].reshape(PAIRS, LANES), power[:, part].reshape(PAIRS, 1))
        payload = fixed(jnp.concatenate([out[:, part].reshape(PAIRS, HD), top], axis=0))
        for z in range(out_ref.shape[0] // 2):
            flat[2 * z + c] = payload


def merge_kernel(in_ref, out_ref):
    flat = in_ref.reshape(in_ref.shape[0], PAY, HD)
    halves = [range(0, 8), range(8, 16)]
    heads = [read_headers(flat, half) for half in halves]
    peak = jnp.max(jnp.maximum(heads[0][0], heads[1][0]), axis=0, keepdims=True)
    weights = [jnp.exp(lse - peak) for lse, _ in heads]
    mass = jnp.sum(weights[0] + weights[1], axis=0, keepdims=True)
    lse = peak + jnp.log(mass)
    weights = [w * scale / mass for w, (_, scale) in zip(weights, heads)]
    groups = BLOCKS
    rows = by_block([t for w in weights for t in (w, pltpu.roll(w, 4, 0))])
    at = iota((PAIRS, LANES), 1) % PAIRS == iota((PAIRS, LANES), 0)
    spread = jnp.concatenate(
        [jnp.where(at, rows[g : g + 1], 0.0) for g in range(groups)], axis=1
    )
    members = [k * groups + g for g in range(groups) for k in range(BLOCKS)]
    out = split_dot(spread, stack(flat, members))
    power = power_of(out)
    payload = fixed(jnp.concatenate([coded(out, power), header(lse, power)], axis=0))
    sent = out_ref.reshape(out_ref.shape[0], PAY, HD)
    for i in range(out_ref.shape[0]):
        sent[i] = payload


def project_kernel(in_ref, w_ref, proj_ref, mass_ref):
    flat = in_ref.reshape(in_ref.shape[0], PAY, HD)
    groups = in_ref.shape[0] // BLOCKS
    heads = [read_headers(flat, range(groups * y, groups * (y + 1))) for y in range(BLOCKS)]
    peak = functools.reduce(jnp.maximum, [lse for lse, _ in heads])
    weights = [jnp.exp(lse - peak) for lse, _ in heads]
    mass = functools.reduce(jnp.add, weights)
    lse = peak + jnp.log(mass)
    weights = by_block([w * scale / mass for w, (_, scale) in zip(weights, heads)])
    pair = iota((PAIRS, LANES), 0)
    at = lax.rem(iota((PAIRS, LANES), 1), PAIRS) == lax.rem(pair, ROWS) * HALF + pair // ROWS
    heads = []
    for g in range(groups):
        out = split_dot(jnp.where(at, weights[g : g + 1], 0.0), stack(flat, [groups * y + g for y in range(BLOCKS)]))
        heads.extend(out[ROWS * h : ROWS * (h + 1)] for h in range(HALF))
    attended = jnp.concatenate(heads, axis=1).astype(jnp.bfloat16)
    proj_ref[...] = lax.dot_general(
        attended, w_ref[...], (((1,), (1,)), ((), ())), preferred_element_type=jnp.float32
    )
    sub, lane = iota((8, LANES), 0), iota((8, LANES), 1)
    result = jnp.zeros((8, LANES), jnp.float32)
    for c in range(2):
        own = jnp.sum(
            jnp.where(sub == lax.axis_index("x") * 2 + c, lse, 0.0), axis=0, keepdims=True
        )
        own = jnp.broadcast_to(own, (8, LANES))
        for r in range(ROWS):
            shifted = pltpu.roll(own, (LANES + c * HALF - r * HALF) % LANES, 1)
            result = jnp.where((sub == r) & (lane // HALF == c), shifted, result)
    mass_ref[...] = result[:ROWS, :GROUP]


def shards(queries, keys, values, lengths, span_map, w_out):
    slots = span_map.shape[0]
    z, y, x = lax.axis_size("z"), lax.axis_size("y"), lax.axis_size("x")
    f32, bf16 = jnp.float32, jnp.bfloat16
    cache = (slots, SPAN, HD)
    inputs = (queries, lengths, span_map, keys.reshape(cache), values.reshape(cache))
    inputs = [pltpu.with_memory_space_constraint(x, pltpu.HBM) for x in inputs]
    part = pl.pallas_call(
        attend_kernel,
        out_shape=pltpu.VMEM((z * 2, PAY // 2, 2, HD), jnp.int16),
        in_specs=[HBM] * 5,
        out_specs=VMEM,
        scratch_shapes=[
            pltpu.VMEM((ROWS, GROUP, HD), bf16),
            pltpu.SMEM((ROWS,), jnp.int32),
            pltpu.SMEM((slots,), jnp.int32),
            pltpu.VMEM(cache, bf16),
            pltpu.VMEM(cache, bf16),
            pltpu.VMEM((slots, GROUP, SPAN), f32),
            pltpu.VMEM((ROWS, GROUP, LANES), f32),
            pltpu.VMEM((ROWS, GROUP, LANES), f32),
            pltpu.VMEM((ROWS, GROUP, HD), f32),
            pltpu.SemaphoreType.DMA((3,)),
            pltpu.SemaphoreType.DMA((len(KEY_PARTS),)),
            pltpu.SemaphoreType.DMA((len(VALUE_PARTS),)),
        ],
        compiler_params=pltpu.CompilerParams(vmem_limit_bytes=24 * 2**20),
        name="attend",
    )(*inputs)
    part = lax.all_to_all(part, ("z", "core"), 0, 0, tiled=True)
    part = pl.pallas_call(
        merge_kernel,
        out_shape=jax.ShapeDtypeStruct((y * x * 2, PAY // 2, 2, HD), jnp.int16),
        in_specs=[VMEM],
        out_specs=VMEM,
        compiler_params=pltpu.CompilerParams(vmem_limit_bytes=8 * 2**20),
        name="merge",
    )(part)
    part = lax.all_to_all(part, ("y", "x", "core"), 0, 0, tiled=True)
    return pl.pallas_call(
        project_kernel,
        out_shape=(
            jax.ShapeDtypeStruct((ROWS, w_out.shape[1]), f32),
            jax.ShapeDtypeStruct((ROWS, GROUP), f32),
        ),
        in_specs=[VMEM, VMEM],
        out_specs=(VMEM, VMEM),
        compiler_params=pltpu.CompilerParams(vmem_limit_bytes=8 * 2**20),
        name="project",
    )(part, w_out.T)


def solution(mesh):
    fine = Mesh(mesh.devices.reshape(8, 4, 2, 4), ("z", "y", "core", "x"))
    ctx = ("z", "y", "core")
    placed = (
        P(None, "x", None),
        P(ctx, "x", None, None),
        P(ctx, "x", None, None),
        P(),
        P(ctx),
        P(None, ctx),
    )
    return jax.shard_map(
        shards,
        mesh=fine,
        in_specs=placed,
        out_specs=(P(None, ctx), P(None, "x")),
        check_vma=False,
    )
```

```python
import functools
import math

import jax
import jax.numpy as jnp
from jax import lax
from jax.experimental import pallas as pl
from jax.experimental.pallas import tpu as pltpu
from jax.sharding import Mesh, PartitionSpec as P

ROWS, HD, GROUP, SPAN, CPR = 4, 128, 16, 512, 512
HALF = GROUP // 2
PAIRS = ROWS * HALF
PAY = PAIRS + 2
LANES = 128
BLOCKS = LANES // PAIRS
FLOOR = -1e30
NOTHING = -32000.0
TINY = 2.0**-110
STEPS = 32760.0
SCALE = 1.0 / math.sqrt(HD)
LOG2E = math.log2(math.e)
KEY_PARTS = (16, 16)
VALUE_PARTS = (16, 16)

VMEM = pl.BlockSpec(memory_space=pltpu.VMEM)
HBM = pl.BlockSpec(memory_space=pltpu.HBM)


def iota(shape, axis):
    return lax.broadcasted_iota(jnp.int32, shape, axis)


def fixed(x):
    return x.astype(jnp.int32).astype(jnp.int16)


def header(lse, power):
    whole = jnp.floor(lse)
    rest = (lse - whole) * 32768.0
    first = jnp.floor(rest)
    second = jnp.floor((rest - first) * 32768.0)
    shape = (PAIRS, LANES)
    block = iota(shape, 1) // PAIRS
    kind = jnp.where(block == 0, whole, jnp.where(block == 1, first, second))
    kind = jnp.where(block == 3, power, kind)
    row = jnp.sum(
        jnp.where(iota(shape, 1) % PAIRS == iota(shape, 0), kind, 0.0), axis=0, keepdims=True
    )
    return jnp.broadcast_to(row, (2, LANES))


def read_headers(flat, members):
    rows = [flat[i, PAIRS:PAY].astype(jnp.int32).astype(jnp.float32)[0:1] for i in members]
    rows = jnp.concatenate(rows, axis=0)
    block = iota(rows.shape, 1) // PAIRS
    unit = jnp.where(block == 0, 1.0, jnp.where(block == 1, 2.0**-15, 2.0**-30))
    lse = over_blocks(jnp.where(block == 3, 0.0, rows * unit), jnp.add)
    scale = over_blocks(jnp.where(block == 3, rows, 0.0), jnp.add)
    return lse, jnp.exp2(scale * (1.0 / 256.0)) * (1.0 / STEPS)


def by_block(tiles):
    block = iota(tiles[0].shape, 1) // PAIRS
    out = tiles[0]
    for k in range(1, BLOCKS):
        out = jnp.where(block == k, tiles[k], out)
    return out


def power_of(out):
    largest = jnp.max(jnp.abs(out), axis=-1, keepdims=True)
    return jnp.ceil(jnp.log2(jnp.maximum(largest, TINY)) * 256.0 + 1.0)


def coded(out, power):
    return jnp.round(out * (jnp.exp2(power * (-1.0 / 256.0)) * STEPS))


def weighted_sum(flat, row, members):
    shape = (PAIRS, LANES)
    block = iota(shape, 1) // PAIRS
    spread = jnp.where(iota(shape, 1) % PAIRS == iota(shape, 0), row, 0.0)
    terms = []
    for k, i in enumerate(members):
        column = jnp.sum(jnp.where(block == k, spread, 0.0), axis=1, keepdims=True)
        terms.append(column * flat[i, 0:PAIRS].astype(jnp.int32).astype(jnp.float32))
    return (terms[0] + terms[1]) + (terms[2] + terms[3])


def over_blocks(x, op):
    step = PAIRS
    while step < LANES:
        x = op(x, pltpu.roll(x, step, 1))
        step *= 2
    return x


def attend_kernel(
    q_hbm, len_hbm, map_hbm, k_hbm, v_hbm, out_ref,
    q_ref, len_ref, map_ref, kbuf, vbuf, s_ref, m_ref, l_ref, acc_ref, order, sem, ksem, vsem,
):
    small = [
        pltpu.make_async_copy(source, target, sem.at[i])
        for i, (source, target) in enumerate(
            [(map_hbm, map_ref), (len_hbm, len_ref), (q_hbm, q_ref)]
        )
    ]

    def copies(source, target, sems, sizes):
        at = [sum(sizes[:i]) for i in range(len(sizes))]
        return [range(start, start + size) for start, size in zip(at, sizes)], [
            pltpu.make_async_copy(
                source.at[pl.ds(start, size)], target.at[pl.ds(start, size)], sems.at[i]
            )
            for i, (start, size) in enumerate(zip(at, sizes))
        ]

    kparts, kcopies = copies(k_hbm, kbuf, ksem, KEY_PARTS)
    vparts, vcopies = copies(v_hbm, vbuf, vsem, VALUE_PARTS)
    for copy in small + kcopies:
        copy.start(priority=0)
    for copy in vcopies:
        copy.start(priority=1)
    m_ref[...] = jnp.full(m_ref.shape, FLOOR, jnp.float32)
    l_ref[...] = jnp.zeros_like(l_ref)
    acc_ref[...] = jnp.zeros_like(acc_ref)
    for copy in small:
        copy.wait()

    def place(c):
        span = map_ref[c]
        row = lax.shift_right_logical(span, CPR.bit_length() - 1)
        return row, lax.bitwise_and(span, CPR - 1) * SPAN < len_ref[row]

    def folded(x, op):
        tiles = [x[:, i * LANES : (i + 1) * LANES] for i in range(SPAN // LANES)]
        return op(op(tiles[0], tiles[1]), op(tiles[2], tiles[3]))

    for part, copy in zip(kparts, kcopies):
        copy.wait()
        for c in part:
            row, live = place(c)
            s = lax.dot_general(
                q_ref[row], kbuf[c], (((1,), (1,)), ((), ())), preferred_element_type=jnp.float32
            )
            s_ref[c] = s
            m_ref[row] = jnp.maximum(
                m_ref[row], jnp.where(live, folded(s, jnp.maximum), FLOOR)
            )
    m_ref[...] = jnp.broadcast_to(jnp.max(m_ref[...], axis=2, keepdims=True), m_ref.shape)

    for part, copy in zip(vparts, vcopies):
        copy.wait()
        for c in part:
            row, live = place(c)
            top = jnp.where(live, m_ref[row], -FLOOR)
            top = jnp.concatenate([top] * (SPAN // LANES), axis=1)
            p = jnp.exp2((s_ref[c] - top) * (SCALE * LOG2E)).astype(jnp.bfloat16)
            l_ref[row] += folded(p.astype(jnp.float32), jnp.add)
            acc_ref[row] += jnp.dot(p, vbuf[c], preferred_element_type=jnp.float32)

    l = jnp.broadcast_to(jnp.sum(l_ref[...], axis=2, keepdims=True), l_ref.shape)
    some = l > 0.0
    safe = jnp.where(some, l, 1.0)
    lse = jnp.where(some, m_ref[...] * SCALE + jnp.log(safe), NOTHING)
    out = acc_ref[...] / safe
    power = power_of(out)
    out = coded(out, power)
    flat = out_ref.reshape(out_ref.shape[0], PAY, HD)
    for c in range(2):
        for i, values in enumerate((out, lse, jnp.broadcast_to(power, out.shape))):
            for r in range(ROWS):
                order[c, i, pl.ds(r, HALF, stride=ROWS), :] = values[r, c * HALF : (c + 1) * HALF]
        payload = jnp.concatenate([order[c, 0], header(order[c, 1], order[c, 2])], axis=0)
        payload = fixed(payload)
        for z in range(out_ref.shape[0] // 2):
            flat[2 * z + c] = payload


def merge_kernel(in_ref, out_ref):
    flat = in_ref.reshape(in_ref.shape[0], PAY, HD)
    halves = [range(0, 8), range(8, 16)]
    heads = [read_headers(flat, half) for half in halves]
    peak = jnp.max(jnp.maximum(heads[0][0], heads[1][0]), axis=0, keepdims=True)
    weights = [jnp.exp(lse - peak) for lse, _ in heads]
    mass = jnp.sum(weights[0] + weights[1], axis=0, keepdims=True)
    lse = peak + jnp.log(mass)
    weights = [w * scale / mass for w, (_, scale) in zip(weights, heads)]
    groups = BLOCKS
    rows = by_block([t for w in weights for t in (w, pltpu.roll(w, 4, 0))])
    parts = [
        weighted_sum(flat, rows[g : g + 1], [k * groups + g for k in range(BLOCKS)])
        for g in range(groups)
    ]
    out = (parts[0] + parts[1]) + (parts[2] + parts[3])
    power = power_of(out)
    payload = fixed(jnp.concatenate([coded(out, power), header(lse, power)], axis=0))
    sent = out_ref.reshape(out_ref.shape[0], PAY, HD)
    for i in range(out_ref.shape[0]):
        sent[i] = payload


def project_kernel(in_ref, w_ref, proj_ref, mass_ref):
    flat = in_ref.reshape(in_ref.shape[0], PAY, HD)
    groups = in_ref.shape[0] // BLOCKS
    heads = [read_headers(flat, range(groups * y, groups * (y + 1))) for y in range(BLOCKS)]
    peak = functools.reduce(jnp.maximum, [lse for lse, _ in heads])
    weights = [jnp.exp(lse - peak) for lse, _ in heads]
    mass = functools.reduce(jnp.add, weights)
    lse = peak + jnp.log(mass)
    weights = by_block([w * scale / mass for w, (_, scale) in zip(weights, heads)])
    heads = []
    for g in range(groups):
        out = weighted_sum(
            flat, weights[g : g + 1], [groups * y + g for y in range(BLOCKS)]
        )
        heads.extend(out[ROWS * h : ROWS * (h + 1)] for h in range(HALF))
    attended = jnp.concatenate(heads, axis=1).astype(jnp.bfloat16)
    proj_ref[...] = lax.dot_general(
        attended, w_ref[...], (((1,), (1,)), ((), ())), preferred_element_type=jnp.float32
    )
    pair, lane = iota((PAIRS, LANES), 0), iota((PAIRS, LANES), 1)
    table = jnp.zeros((PAIRS, LANES), jnp.float32)
    for c in range(2):
        mine = iota(lse.shape, 0) == lax.axis_index("x") * 2 + c
        own = jnp.sum(jnp.where(mine, lse, 0.0), axis=0, keepdims=True)
        column = jnp.sum(jnp.where(lane == pair, own, 0.0), axis=1, keepdims=True)
        table = jnp.where(lane == c * HALF + pair // ROWS, column, table)
    table = sum(table[8 * i : 8 * (i + 1)] for i in range(PAIRS // 8))
    mass_ref[...] = (table[:ROWS] + table[ROWS:])[:, :GROUP]


def shards(queries, keys, values, lengths, span_map, w_out):
    slots = span_map.shape[0]
    z, y, x = lax.axis_size("z"), lax.axis_size("y"), lax.axis_size("x")
    f32, bf16 = jnp.float32, jnp.bfloat16
    cache = (slots, SPAN, HD)
    inputs = (queries, lengths, span_map, keys.reshape(cache), values.reshape(cache))
    inputs = [pltpu.with_memory_space_constraint(x, pltpu.HBM) for x in inputs]
    part = pl.pallas_call(
        attend_kernel,
        out_shape=pltpu.VMEM((z * 2, PAY // 2, 2, HD), jnp.int16),
        in_specs=[HBM] * 5,
        out_specs=VMEM,
        scratch_shapes=[
            pltpu.VMEM((ROWS, GROUP, HD), bf16),
            pltpu.SMEM((ROWS,), jnp.int32),
            pltpu.SMEM((slots,), jnp.int32),
            pltpu.VMEM(cache, bf16),
            pltpu.VMEM(cache, bf16),
            pltpu.VMEM((slots, GROUP, SPAN), f32),
            pltpu.VMEM((ROWS, GROUP, LANES), f32),
            pltpu.VMEM((ROWS, GROUP, LANES), f32),
            pltpu.VMEM((ROWS, GROUP, HD), f32),
            pltpu.VMEM((2, 3, PAIRS, LANES), f32),
            pltpu.SemaphoreType.DMA((3,)),
            pltpu.SemaphoreType.DMA((len(KEY_PARTS),)),
            pltpu.SemaphoreType.DMA((len(VALUE_PARTS),)),
        ],
        compiler_params=pltpu.CompilerParams(vmem_limit_bytes=24 * 2**20),
        name="attend",
    )(*inputs)
    part = lax.all_to_all(part, ("z", "core"), 0, 0, tiled=True)
    part = pl.pallas_call(
        merge_kernel,
        out_shape=jax.ShapeDtypeStruct((y * x * 2, PAY // 2, 2, HD), jnp.int16),
        in_specs=[VMEM],
        out_specs=VMEM,
        compiler_params=pltpu.CompilerParams(vmem_limit_bytes=8 * 2**20),
        name="merge",
    )(part)
    part = lax.all_to_all(part, ("y", "x", "core"), 0, 0, tiled=True)
    return pl.pallas_call(
        project_kernel,
        out_shape=(
            jax.ShapeDtypeStruct((ROWS, w_out.shape[1]), f32),
            jax.ShapeDtypeStruct((ROWS, GROUP), f32),
        ),
        in_specs=[VMEM, VMEM],
        out_specs=(VMEM, VMEM),
        compiler_params=pltpu.CompilerParams(vmem_limit_bytes=8 * 2**20),
        name="project",
    )(part, w_out.T)


def solution(mesh):
    fine = Mesh(mesh.devices.reshape(8, 4, 2, 4), ("z", "y", "core", "x"))
    ctx = ("z", "y", "core")
    placed = (
        P(None, "x", None),
        P(ctx, "x", None, None),
        P(ctx, "x", None, None),
        P(),
        P(ctx),
        P(None, ctx),
    )
    return jax.shard_map(
        shards,
        mesh=fine,
        in_specs=placed,
        out_specs=(P(None, ctx), P(None, "x")),
        check_vma=False,
    )
```

```python
import functools
import math

import jax
import jax.numpy as jnp
from jax import lax
from jax.experimental import pallas as pl
from jax.experimental.pallas import tpu as pltpu
from jax.sharding import Mesh, PartitionSpec as P

ROWS, HD, GROUP, SPAN, CPR = 4, 128, 16, 512, 512
HALF = GROUP // 2
PAIRS = ROWS * HALF
PAY = PAIRS + 2
LANES = 128
BLOCKS = LANES // PAIRS
FLOOR = -1e30
NOTHING = -32000.0
TINY = 2.0**-110
STEPS = 32760.0
SCALE = 1.0 / math.sqrt(HD)
LOG2E = math.log2(math.e)
KEY_PARTS = (16, 16)
VALUE_PARTS = (16, 16)

VMEM = pl.BlockSpec(memory_space=pltpu.VMEM)
HBM = pl.BlockSpec(memory_space=pltpu.HBM)


def iota(shape, axis):
    return lax.broadcasted_iota(jnp.int32, shape, axis)


def fixed(x):
    return x.astype(jnp.int32).astype(jnp.int16)


def header(lse, power):
    whole = jnp.floor(lse)
    rest = (lse - whole) * 32768.0
    first = jnp.minimum(jnp.floor(rest), 32767.0)
    second = jnp.minimum(jnp.floor((rest - first) * 32768.0), 32767.0)
    shape = (PAIRS, LANES)
    block = iota(shape, 1) // PAIRS
    kind = jnp.where(block == 0, whole, jnp.where(block == 1, first, second))
    kind = jnp.where(block == 3, power, kind)
    row = jnp.sum(
        jnp.where(iota(shape, 1) % PAIRS == iota(shape, 0), kind, 0.0), axis=0, keepdims=True
    )
    return jnp.broadcast_to(row, (2, LANES))


def read_headers(flat, members):
    rows = [flat[i, PAIRS:PAY].astype(jnp.int32).astype(jnp.float32)[0:1] for i in members]
    rows = jnp.concatenate(rows, axis=0)
    block = iota(rows.shape, 1) // PAIRS
    unit = jnp.where(block == 0, 1.0, jnp.where(block == 1, 2.0**-15, 2.0**-30))
    lse = over_blocks(jnp.where(block == 3, 0.0, rows * unit), jnp.add)
    scale = over_blocks(jnp.where(block == 3, rows, 0.0), jnp.add)
    return lse, jnp.exp2(scale * (1.0 / 256.0)) * (1.0 / STEPS)


def by_block(tiles):
    block = iota(tiles[0].shape, 1) // PAIRS
    out = tiles[0]
    for k in range(1, BLOCKS):
        out = jnp.where(block == k, tiles[k], out)
    return out


def power_of(out):
    largest = jnp.max(jnp.abs(out), axis=-1, keepdims=True)
    return jnp.ceil(jnp.log2(jnp.maximum(largest, TINY)) * 256.0 + 1.0)


def coded(out, power):
    return jnp.round(out * (jnp.exp2(power * (-1.0 / 256.0)) * STEPS))


def weighted_sum(flat, row, members):
    shape = (PAIRS, LANES)
    block = iota(shape, 1) // PAIRS
    spread = jnp.where(iota(shape, 1) % PAIRS == iota(shape, 0), row, 0.0)
    terms = []
    for k, i in enumerate(members):
        column = jnp.sum(jnp.where(block == k, spread, 0.0), axis=1, keepdims=True)
        terms.append(column * flat[i, 0:PAIRS].astype(jnp.int32).astype(jnp.float32))
    return (terms[0] + terms[1]) + (terms[2] + terms[3])


def over_blocks(x, op):
    step = PAIRS
    while step < LANES:
        x = op(x, pltpu.roll(x, step, 1))
        step *= 2
    return x


def attend_kernel(
    q_hbm, len_hbm, map_hbm, k_hbm, v_hbm, out_ref,
    q_ref, len_ref, map_ref, kbuf, vbuf, s_ref, m_ref, l_ref, acc_ref, order, sem, ksem, vsem,
):
    small = [
        pltpu.make_async_copy(source, target, sem.at[i])
        for i, (source, target) in enumerate(
            [(map_hbm, map_ref), (len_hbm, len_ref), (q_hbm, q_ref)]
        )
    ]

    def copies(source, target, sems, sizes):
        at = [sum(sizes[:i]) for i in range(len(sizes))]
        return [range(start, start + size) for start, size in zip(at, sizes)], [
            pltpu.make_async_copy(
                source.at[pl.ds(start, size)], target.at[pl.ds(start, size)], sems.at[i]
            )
            for i, (start, size) in enumerate(zip(at, sizes))
        ]

    kparts, kcopies = copies(k_hbm, kbuf, ksem, KEY_PARTS)
    vparts, vcopies = copies(v_hbm, vbuf, vsem, VALUE_PARTS)
    for copy in small + kcopies:
        copy.start(priority=0)
    for copy in vcopies:
        copy.start(priority=1)
    m_ref[...] = jnp.full(m_ref.shape, FLOOR, jnp.float32)
    l_ref[...] = jnp.zeros_like(l_ref)
    acc_ref[...] = jnp.zeros_like(acc_ref)
    for copy in small:
        copy.wait()

    def place(c):
        span = map_ref[c]
        row = lax.shift_right_logical(span, CPR.bit_length() - 1)
        return row, lax.bitwise_and(span, CPR - 1) * SPAN < len_ref[row]

    def folded(x, op):
        tiles = [x[:, i * LANES : (i + 1) * LANES] for i in range(SPAN // LANES)]
        return op(op(tiles[0], tiles[1]), op(tiles[2], tiles[3]))

    for part, copy in zip(kparts, kcopies):
        copy.wait()
        for c in part:
            row, live = place(c)
            s = lax.dot_general(
                q_ref[row], kbuf[c], (((1,), (1,)), ((), ())), preferred_element_type=jnp.float32
            )
            s_ref[c] = s
            m_ref[row] = jnp.maximum(
                m_ref[row], jnp.where(live, folded(s, jnp.maximum), FLOOR)
            )
    m_ref[...] = jnp.broadcast_to(jnp.max(m_ref[...], axis=2, keepdims=True), m_ref.shape)

    for part, copy in zip(vparts, vcopies):
        copy.wait()
        for c in part:
            row, live = place(c)
            top = jnp.where(live, m_ref[row], -FLOOR)
            top = jnp.concatenate([top] * (SPAN // LANES), axis=1)
            p = jnp.exp2((s_ref[c] - top) * (SCALE * LOG2E)).astype(jnp.bfloat16)
            l_ref[row] += folded(p.astype(jnp.float32), jnp.add)
            acc_ref[row] += jnp.dot(p, vbuf[c], preferred_element_type=jnp.float32)

    l = jnp.broadcast_to(jnp.sum(l_ref[...], axis=2, keepdims=True), l_ref.shape)
    some = l > 0.0
    safe = jnp.where(some, l, 1.0)
    lse = jnp.where(some, m_ref[...] * SCALE + jnp.log(safe), NOTHING)
    out = acc_ref[...] / safe
    power = power_of(out)
    out = coded(out, power)
    flat = out_ref.reshape(out_ref.shape[0], PAY, HD)
    for c in range(2):
        for i, values in enumerate((out, lse, jnp.broadcast_to(power, out.shape))):
            for r in range(ROWS):
                order[c, i, pl.ds(r, HALF, stride=ROWS), :] = values[r, c * HALF : (c + 1) * HALF]
        payload = jnp.concatenate([order[c, 0], header(order[c, 1], order[c, 2])], axis=0)
        payload = fixed(payload)
        for z in range(out_ref.shape[0] // 2):
            flat[2 * z + c] = payload


def merge_kernel(in_ref, out_ref):
    flat = in_ref.reshape(in_ref.shape[0], PAY, HD)
    halves = [range(0, 8), range(8, 16)]
    heads = [read_headers(flat, half) for half in halves]
    peak = jnp.max(jnp.maximum(heads[0][0], heads[1][0]), axis=0, keepdims=True)
    weights = [jnp.exp(lse - peak) for lse, _ in heads]
    mass = jnp.sum(weights[0] + weights[1], axis=0, keepdims=True)
    lse = peak + jnp.log(mass)
    weights = [w * scale / mass for w, (_, scale) in zip(weights, heads)]
    groups = BLOCKS
    rows = by_block([t for w in weights for t in (w, pltpu.roll(w, 4, 0))])
    parts = [
        weighted_sum(flat, rows[g : g + 1], [k * groups + g for k in range(BLOCKS)])
        for g in range(groups)
    ]
    out = (parts[0] + parts[1]) + (parts[2] + parts[3])
    power = power_of(out)
    payload = fixed(jnp.concatenate([coded(out, power), header(lse, power)], axis=0))
    sent = out_ref.reshape(out_ref.shape[0], PAY, HD)
    for i in range(out_ref.shape[0]):
        sent[i] = payload


def project_kernel(in_ref, w_ref, proj_ref, mass_ref):
    flat = in_ref.reshape(in_ref.shape[0], PAY, HD)
    groups = in_ref.shape[0] // BLOCKS
    heads = [read_headers(flat, range(groups * y, groups * (y + 1))) for y in range(BLOCKS)]
    peak = functools.reduce(jnp.maximum, [lse for lse, _ in heads])
    weights = [jnp.exp(lse - peak) for lse, _ in heads]
    mass = functools.reduce(jnp.add, weights)
    lse = peak + jnp.log(mass)
    weights = by_block([w * scale / mass for w, (_, scale) in zip(weights, heads)])
    heads = []
    for g in range(groups):
        out = weighted_sum(
            flat, weights[g : g + 1], [groups * y + g for y in range(BLOCKS)]
        )
        heads.extend(out[ROWS * h : ROWS * (h + 1)] for h in range(HALF))
    attended = jnp.concatenate(heads, axis=1).astype(jnp.bfloat16)
    proj_ref[...] = lax.dot_general(
        attended, w_ref[...], (((1,), (1,)), ((), ())), preferred_element_type=jnp.float32
    )
    pair, lane = iota((PAIRS, LANES), 0), iota((PAIRS, LANES), 1)
    table = jnp.zeros((PAIRS, LANES), jnp.float32)
    for c in range(2):
        mine = iota(lse.shape, 0) == lax.axis_index("x") * 2 + c
        own = jnp.sum(jnp.where(mine, lse, 0.0), axis=0, keepdims=True)
        column = jnp.sum(jnp.where(lane == pair, own, 0.0), axis=1, keepdims=True)
        table = jnp.where(lane == c * HALF + pair // ROWS, column, table)
    table = sum(table[8 * i : 8 * (i + 1)] for i in range(PAIRS // 8))
    mass_ref[...] = (table[:ROWS] + table[ROWS:])[:, :GROUP]


def shards(queries, keys, values, lengths, span_map, w_out):
    slots = span_map.shape[0]
    z, y, x = lax.axis_size("z"), lax.axis_size("y"), lax.axis_size("x")
    f32, bf16 = jnp.float32, jnp.bfloat16
    cache = (slots, SPAN, HD)
    inputs = (queries, lengths, span_map, keys.reshape(cache), values.reshape(cache))
    inputs = [pltpu.with_memory_space_constraint(x, pltpu.HBM) for x in inputs]
    part = pl.pallas_call(
        attend_kernel,
        out_shape=pltpu.VMEM((z * 2, PAY // 2, 2, HD), jnp.int16),
        in_specs=[HBM] * 5,
        out_specs=VMEM,
        scratch_shapes=[
            pltpu.VMEM((ROWS, GROUP, HD), bf16),
            pltpu.SMEM((ROWS,), jnp.int32),
            pltpu.SMEM((slots,), jnp.int32),
            pltpu.VMEM(cache, bf16),
            pltpu.VMEM(cache, bf16),
            pltpu.VMEM((slots, GROUP, SPAN), f32),
            pltpu.VMEM((ROWS, GROUP, LANES), f32),
            pltpu.VMEM((ROWS, GROUP, LANES), f32),
            pltpu.VMEM((ROWS, GROUP, HD), f32),
            pltpu.VMEM((2, 3, PAIRS, LANES), f32),
            pltpu.SemaphoreType.DMA((3,)),
            pltpu.SemaphoreType.DMA((len(KEY_PARTS),)),
            pltpu.SemaphoreType.DMA((len(VALUE_PARTS),)),
        ],
        compiler_params=pltpu.CompilerParams(vmem_limit_bytes=24 * 2**20),
        name="attend",
    )(*inputs)
    part = lax.all_to_all(part, ("z", "core"), 0, 0, tiled=True)
    part = pl.pallas_call(
        merge_kernel,
        out_shape=jax.ShapeDtypeStruct((y * x * 2, PAY // 2, 2, HD), jnp.int16),
        in_specs=[VMEM],
        out_specs=VMEM,
        compiler_params=pltpu.CompilerParams(vmem_limit_bytes=8 * 2**20),
        name="merge",
    )(part)
    part = lax.all_to_all(part, ("y", "x", "core"), 0, 0, tiled=True)
    return pl.pallas_call(
        project_kernel,
        out_shape=(
            jax.ShapeDtypeStruct((ROWS, w_out.shape[1]), f32),
            jax.ShapeDtypeStruct((ROWS, GROUP), f32),
        ),
        in_specs=[VMEM, VMEM],
        out_specs=(VMEM, VMEM),
        compiler_params=pltpu.CompilerParams(vmem_limit_bytes=8 * 2**20),
        name="project",
    )(part, w_out.T)


def solution(mesh):
    fine = Mesh(mesh.devices.reshape(8, 4, 2, 4), ("z", "y", "core", "x"))
    ctx = ("z", "y", "core")
    placed = (
        P(None, "x", None),
        P(ctx, "x", None, None),
        P(ctx, "x", None, None),
        P(),
        P(ctx),
        P(None, ctx),
    )
    return jax.shard_map(
        shards,
        mesh=fine,
        in_specs=placed,
        out_specs=(P(None, ctx), P(None, "x")),
        check_vma=False,
    )
```

```python
import functools
import math

import jax
import jax.numpy as jnp
from jax import lax
from jax.experimental import pallas as pl
from jax.experimental.pallas import tpu as pltpu
from jax.sharding import Mesh, PartitionSpec as P

ROWS, HD, GROUP, SPAN, CPR = 4, 128, 16, 512, 512
HALF = GROUP // 2
PAIRS = ROWS * HALF
PAY = PAIRS + 2
LANES = 128
BLOCKS = LANES // PAIRS
FLOOR = -1e30
NOTHING = -32000.0
TINY = 2.0**-110
STEPS = 32760.0
SCALE = 1.0 / math.sqrt(HD)
LOG2E = math.log2(math.e)
KEY_PARTS = (16, 16)
VALUE_PARTS = (16, 16)

VMEM = pl.BlockSpec(memory_space=pltpu.VMEM)
HBM = pl.BlockSpec(memory_space=pltpu.HBM)


def iota(shape, axis):
    return lax.broadcasted_iota(jnp.int32, shape, axis)


def fixed(x):
    return x.astype(jnp.int32).astype(jnp.int16)


def header(lse, power):
    whole = jnp.floor(lse)
    rest = (lse - whole) * 32768.0
    first = jnp.minimum(jnp.floor(rest), 32767.0)
    second = jnp.minimum(jnp.floor((rest - first) * 32768.0), 32767.0)
    shape = (PAIRS, LANES)
    block = iota(shape, 1) // PAIRS
    kind = jnp.where(block == 0, whole, jnp.where(block == 1, first, second))
    kind = jnp.where(block == 3, power, kind)
    row = jnp.sum(
        jnp.where(iota(shape, 1) % PAIRS == iota(shape, 0), kind, 0.0), axis=0, keepdims=True
    )
    return jnp.broadcast_to(row, (2, LANES))


def read_headers(flat, members):
    rows = [flat[i, PAIRS:PAY].astype(jnp.int32).astype(jnp.float32)[0:1] for i in members]
    rows = jnp.concatenate(rows, axis=0)
    block = iota(rows.shape, 1) // PAIRS
    unit = jnp.where(block == 0, 1.0, jnp.where(block == 1, 2.0**-15, 2.0**-30))
    lse = over_blocks(jnp.where(block == 3, 0.0, rows * unit), jnp.add)
    scale = over_blocks(jnp.where(block == 3, rows, 0.0), jnp.add)
    return lse, jnp.exp2(scale * (1.0 / 256.0)) * (1.0 / STEPS)


def by_block(tiles):
    block = iota(tiles[0].shape, 1) // PAIRS
    out = tiles[0]
    for k in range(1, BLOCKS):
        out = jnp.where(block == k, tiles[k], out)
    return out


def power_of(out):
    largest = jnp.max(jnp.abs(out), axis=-1, keepdims=True)
    return jnp.ceil(jnp.log2(jnp.maximum(largest, TINY)) * 256.0 + 1.0)


def coded(out, power):
    return jnp.round(out * (jnp.exp2(power * (-1.0 / 256.0)) * STEPS))


def weighted_sum(flat, row, members):
    shape = (PAIRS, LANES)
    block = iota(shape, 1) // PAIRS
    spread = jnp.where(iota(shape, 1) % PAIRS == iota(shape, 0), row, 0.0)
    terms = []
    for k, i in enumerate(members):
        column = jnp.sum(jnp.where(block == k, spread, 0.0), axis=1, keepdims=True)
        terms.append(column * flat[i, 0:PAIRS].astype(jnp.int32).astype(jnp.float32))
    return (terms[0] + terms[1]) + (terms[2] + terms[3])


def over_blocks(x, op):
    step = PAIRS
    while step < LANES:
        x = op(x, pltpu.roll(x, step, 1))
        step *= 2
    return x


def attend_kernel(
    q_hbm, len_hbm, map_hbm, k_hbm, v_hbm, out_ref,
    q_ref, len_ref, map_ref, kbuf, vbuf, s_ref, m_ref, l_ref, acc_ref, order, sem, ksem, vsem,
):
    small = [
        pltpu.make_async_copy(source, target, sem.at[i])
        for i, (source, target) in enumerate(
            [(map_hbm, map_ref), (len_hbm, len_ref), (q_hbm, q_ref)]
        )
    ]

    def copies(source, target, sems, sizes):
        at = [sum(sizes[:i]) for i in range(len(sizes))]
        return [range(start, start + size) for start, size in zip(at, sizes)], [
            pltpu.make_async_copy(
                source.at[pl.ds(start, size)], target.at[pl.ds(start, size)], sems.at[i]
            )
            for i, (start, size) in enumerate(zip(at, sizes))
        ]

    kparts, kcopies = copies(k_hbm, kbuf, ksem, KEY_PARTS)
    vparts, vcopies = copies(v_hbm, vbuf, vsem, VALUE_PARTS)
    for copy in small + kcopies:
        copy.start(priority=0)
    for copy in vcopies:
        copy.start(priority=1)
    m_ref[...] = jnp.full(m_ref.shape, FLOOR, jnp.float32)
    l_ref[...] = jnp.zeros_like(l_ref)
    acc_ref[...] = jnp.zeros_like(acc_ref)
    for copy in small:
        copy.wait()

    def place(c):
        span = map_ref[c]
        row = lax.shift_right_logical(span, CPR.bit_length() - 1)
        return row, lax.bitwise_and(span, CPR - 1) * SPAN < len_ref[row]

    def folded(x, op):
        tiles = [x[:, i * LANES : (i + 1) * LANES] for i in range(SPAN // LANES)]
        return op(op(tiles[0], tiles[1]), op(tiles[2], tiles[3]))

    for part, copy in zip(kparts, kcopies):
        copy.wait()
        for c in part:
            row, live = place(c)
            s = lax.dot_general(
                q_ref[row], kbuf[c], (((1,), (1,)), ((), ())), preferred_element_type=jnp.float32
            )
            s_ref[c] = s
            m_ref[row] = jnp.maximum(
                m_ref[row], jnp.where(live, folded(s, jnp.maximum), FLOOR)
            )
    m_ref[...] = jnp.broadcast_to(jnp.max(m_ref[...], axis=2, keepdims=True), m_ref.shape)

    for part, copy in zip(vparts, vcopies):
        copy.wait()
        for c in part:
            row, live = place(c)
            top = jnp.where(live, m_ref[row], -FLOOR)
            top = jnp.concatenate([top] * (SPAN // LANES), axis=1)
            p = jnp.exp2((s_ref[c] - top) * (SCALE * LOG2E)).astype(jnp.bfloat16)
            l_ref[row] += folded(p.astype(jnp.float32), jnp.add)
            acc_ref[row] += jnp.dot(p, vbuf[c], preferred_element_type=jnp.float32)

    l = jnp.broadcast_to(jnp.sum(l_ref[...], axis=2, keepdims=True), l_ref.shape)
    some = l > 0.0
    safe = jnp.where(some, l, 1.0)
    lse = jnp.where(some, m_ref[...] * SCALE + jnp.log(safe), NOTHING)
    out = acc_ref[...] / safe
    power = power_of(out)
    out = coded(out, power)
    flat = out_ref.reshape(out_ref.shape[0], PAY, HD)
    for c in range(2):
        for i, values in enumerate((out, lse, jnp.broadcast_to(power, out.shape))):
            for r in range(ROWS):
                order[c, i, pl.ds(r, HALF, stride=ROWS), :] = values[r, c * HALF : (c + 1) * HALF]
        payload = jnp.concatenate([order[c, 0], header(order[c, 1], order[c, 2])], axis=0)
        payload = fixed(payload)
        for z in range(out_ref.shape[0] // 2):
            flat[2 * z + c] = payload


def merge_kernel(in_ref, out_ref):
    flat = in_ref.reshape(in_ref.shape[0], PAY, HD)
    halves = [range(0, 8), range(8, 16)]
    heads = [read_headers(flat, half) for half in halves]
    peak = jnp.max(jnp.maximum(heads[0][0], heads[1][0]), axis=0, keepdims=True)
    weights = [jnp.exp(lse - peak) for lse, _ in heads]
    mass = jnp.sum(weights[0] + weights[1], axis=0, keepdims=True)
    lse = peak + jnp.log(mass)
    weights = [w * scale / mass for w, (_, scale) in zip(weights, heads)]
    groups = BLOCKS
    rows = by_block([t for w in weights for t in (w, pltpu.roll(w, 4, 0))])
    parts = [
        weighted_sum(flat, rows[g : g + 1], [k * groups + g for k in range(BLOCKS)])
        for g in range(groups)
    ]
    out = (parts[0] + parts[1]) + (parts[2] + parts[3])
    power = power_of(out)
    payload = fixed(jnp.concatenate([coded(out, power), header(lse, power)], axis=0))
    sent = out_ref.reshape(out_ref.shape[0], PAY, HD)
    for i in range(out_ref.shape[0]):
        sent[i] = payload


def gather_kernel(in_ref, out_ref):
    flat = in_ref.reshape(in_ref.shape[0], PAY, HD)
    groups = in_ref.shape[0] // BLOCKS
    heads = [read_headers(flat, range(8 * t, 8 * t + 8)) for t in range(2)]
    peak = jnp.maximum(heads[0][0], heads[1][0])
    peak = jnp.maximum(peak, pltpu.roll(peak, 4, 0))
    weights = [jnp.exp(lse - peak) for lse, _ in heads]
    mass = weights[0] + weights[1]
    mass = mass + pltpu.roll(mass, 4, 0)
    weights = [w * scale / mass for w, (_, scale) in zip(weights, heads)]
    rows = by_block([t for w in weights for t in (w, pltpu.roll(w, 4, 0))])
    for g in range(groups):
        out_ref[g * PAIRS : (g + 1) * PAIRS] = weighted_sum(
            flat, rows[g : g + 1], [groups * k + g for k in range(BLOCKS)]
        )
    out_ref[groups * PAIRS : groups * PAIRS + 8] = peak + jnp.log(mass)


def project_kernel(mine_ref, other_ref, w_ref, proj_ref, mass_ref):
    groups = mine_ref.shape[0] // PAIRS
    first = lax.axis_index("core") == 0
    mine, other = mine_ref[...], other_ref[...]
    halves = [jnp.where(first, mine, other), jnp.where(first, other, mine)]
    heads = [
        halves[c][x * PAIRS + ROWS * h : x * PAIRS + ROWS * (h + 1)]
        for x in range(groups)
        for c in range(2)
        for h in range(HALF)
    ]
    attended = jnp.concatenate(heads, axis=1).astype(jnp.bfloat16)
    proj_ref[...] = lax.dot_general(
        attended, w_ref[...], (((1,), (1,)), ((), ())), preferred_element_type=jnp.float32
    )
    pair, lane = iota((PAIRS, LANES), 0), iota((PAIRS, LANES), 1)
    table = jnp.zeros((PAIRS, LANES), jnp.float32)
    for c in range(2):
        lse = halves[c][groups * PAIRS : groups * PAIRS + 8]
        own = jnp.where(iota(lse.shape, 0) == lax.axis_index("x"), lse, 0.0)
        own = jnp.sum(own, axis=0, keepdims=True)
        column = jnp.sum(jnp.where(lane == pair, own, 0.0), axis=1, keepdims=True)
        table = jnp.where(lane == c * HALF + pair // ROWS, column, table)
    table = sum(table[8 * i : 8 * (i + 1)] for i in range(PAIRS // 8))
    mass_ref[...] = (table[:ROWS] + table[ROWS:])[:, :GROUP]


def shards(queries, keys, values, lengths, span_map, w_out):
    slots = span_map.shape[0]
    z, y, x = lax.axis_size("z"), lax.axis_size("y"), lax.axis_size("x")
    f32, bf16 = jnp.float32, jnp.bfloat16
    cache = (slots, SPAN, HD)
    inputs = (queries, lengths, span_map, keys.reshape(cache), values.reshape(cache))
    inputs = [pltpu.with_memory_space_constraint(x, pltpu.HBM) for x in inputs]
    part = pl.pallas_call(
        attend_kernel,
        out_shape=pltpu.VMEM((z * 2, PAY // 2, 2, HD), jnp.int16),
        in_specs=[HBM] * 5,
        out_specs=VMEM,
        scratch_shapes=[
            pltpu.VMEM((ROWS, GROUP, HD), bf16),
            pltpu.SMEM((ROWS,), jnp.int32),
            pltpu.SMEM((slots,), jnp.int32),
            pltpu.VMEM(cache, bf16),
            pltpu.VMEM(cache, bf16),
            pltpu.VMEM((slots, GROUP, SPAN), f32),
            pltpu.VMEM((ROWS, GROUP, LANES), f32),
            pltpu.VMEM((ROWS, GROUP, LANES), f32),
            pltpu.VMEM((ROWS, GROUP, HD), f32),
            pltpu.VMEM((2, 3, PAIRS, LANES), f32),
            pltpu.SemaphoreType.DMA((3,)),
            pltpu.SemaphoreType.DMA((len(KEY_PARTS),)),
            pltpu.SemaphoreType.DMA((len(VALUE_PARTS),)),
        ],
        compiler_params=pltpu.CompilerParams(vmem_limit_bytes=24 * 2**20),
        name="attend",
    )(*inputs)
    part = lax.all_to_all(part, ("z", "core"), 0, 0, tiled=True)
    part = pl.pallas_call(
        merge_kernel,
        out_shape=jax.ShapeDtypeStruct((y * x, PAY // 2, 2, HD), jnp.int16),
        in_specs=[VMEM],
        out_specs=VMEM,
        compiler_params=pltpu.CompilerParams(vmem_limit_bytes=8 * 2**20),
        name="merge",
    )(part)
    part = lax.all_to_all(part, ("y", "x"), 0, 0, tiled=True)
    mine = pl.pallas_call(
        gather_kernel,
        out_shape=pltpu.VMEM((x * PAIRS + 8, HD), f32),
        in_specs=[VMEM],
        out_specs=VMEM,
        compiler_params=pltpu.CompilerParams(vmem_limit_bytes=8 * 2**20),
        name="gather",
    )(part)
    other = lax.ppermute(mine, "core", [(0, 1), (1, 0)])
    return pl.pallas_call(
        project_kernel,
        out_shape=(
            jax.ShapeDtypeStruct((ROWS, w_out.shape[1]), f32),
            jax.ShapeDtypeStruct((ROWS, GROUP), f32),
        ),
        in_specs=[VMEM, VMEM, VMEM],
        out_specs=(VMEM, VMEM),
        compiler_params=pltpu.CompilerParams(vmem_limit_bytes=8 * 2**20),
        name="project",
    )(mine, other, w_out.T)


def solution(mesh):
    fine = Mesh(mesh.devices.reshape(8, 4, 2, 4), ("z", "y", "core", "x"))
    ctx = ("z", "y", "core")
    placed = (
        P(None, "x", None),
        P(ctx, "x", None, None),
        P(ctx, "x", None, None),
        P(),
        P(ctx),
        P(None, ctx),
    )
    return jax.shard_map(
        shards,
        mesh=fine,
        in_specs=placed,
        out_specs=(P(None, ctx), P(None, "x")),
        check_vma=False,
    )
```

```python
import functools
import math

import jax
import jax.numpy as jnp
from jax import lax
from jax.experimental import pallas as pl
from jax.experimental.pallas import tpu as pltpu
from jax.sharding import Mesh, PartitionSpec as P

ROWS, HD, GROUP, SPAN, CPR = 4, 128, 16, 512, 512
HALF = GROUP // 2
PAIRS = ROWS * HALF
PAY = PAIRS + 2
LANES = 128
BLOCKS = LANES // PAIRS
FLOOR = -1e30
NOTHING = -32000.0
TINY = 2.0**-110
STEPS = 32760.0
SCALE = 1.0 / math.sqrt(HD)
LOG2E = math.log2(math.e)
KEY_PARTS = (16, 16)
VALUE_PARTS = (16, 16)

VMEM = pl.BlockSpec(memory_space=pltpu.VMEM)
HBM = pl.BlockSpec(memory_space=pltpu.HBM)


def iota(shape, axis):
    return lax.broadcasted_iota(jnp.int32, shape, axis)


def fixed(x):
    return x.astype(jnp.int32).astype(jnp.int16)


def header(lse, power):
    whole = jnp.floor(lse)
    rest = (lse - whole) * 32768.0
    first = jnp.minimum(jnp.floor(rest), 32767.0)
    second = jnp.minimum(jnp.floor((rest - first) * 32768.0), 32767.0)
    shape = (PAIRS, LANES)
    block = iota(shape, 1) // PAIRS
    kind = jnp.where(block == 0, whole, jnp.where(block == 1, first, second))
    kind = jnp.where(block == 3, power, kind)
    row = jnp.sum(
        jnp.where(iota(shape, 1) % PAIRS == iota(shape, 0), kind, 0.0), axis=0, keepdims=True
    )
    return jnp.broadcast_to(row, (2, LANES))


def read_headers(flat, members):
    rows = [flat[i, PAIRS:PAY].astype(jnp.int32).astype(jnp.float32)[0:1] for i in members]
    rows = jnp.concatenate(rows, axis=0)
    block = iota(rows.shape, 1) // PAIRS
    unit = jnp.where(block == 0, 1.0, jnp.where(block == 1, 2.0**-15, 2.0**-30))
    lse = over_blocks(jnp.where(block == 3, 0.0, rows * unit), jnp.add)
    scale = over_blocks(jnp.where(block == 3, rows, 0.0), jnp.add)
    return lse, jnp.exp2(scale * (1.0 / 256.0)) * (1.0 / STEPS)


def by_block(tiles):
    block = iota(tiles[0].shape, 1) // PAIRS
    out = tiles[0]
    for k in range(1, BLOCKS):
        out = jnp.where(block == k, tiles[k], out)
    return out


def power_of(out):
    largest = jnp.max(jnp.abs(out), axis=-1, keepdims=True)
    return jnp.ceil(jnp.log2(jnp.maximum(largest, TINY)) * 256.0 + 1.0)


def coded(out, power):
    return jnp.round(out * (jnp.exp2(power * (-1.0 / 256.0)) * STEPS))


def weighted_sum(flat, row, members):
    shape = (PAIRS, LANES)
    block = iota(shape, 1) // PAIRS
    spread = jnp.where(iota(shape, 1) % PAIRS == iota(shape, 0), row, 0.0)
    terms = []
    for k, i in enumerate(members):
        column = jnp.sum(jnp.where(block == k, spread, 0.0), axis=1, keepdims=True)
        terms.append(column * flat[i, 0:PAIRS].astype(jnp.int32).astype(jnp.float32))
    return (terms[0] + terms[1]) + (terms[2] + terms[3])


def over_blocks(x, op):
    step = PAIRS
    while step < LANES:
        x = op(x, pltpu.roll(x, step, 1))
        step *= 2
    return x


def attend_kernel(
    q_hbm, len_hbm, map_hbm, k_hbm, v_hbm, out_ref,
    q_ref, len_ref, map_ref, kbuf, vbuf, s_ref, m_ref, l_ref, acc_ref, order, sem, ksem, vsem,
):
    small = [
        pltpu.make_async_copy(source, target, sem.at[i])
        for i, (source, target) in enumerate(
            [(map_hbm, map_ref), (len_hbm, len_ref), (q_hbm, q_ref)]
        )
    ]

    def copies(source, target, sems, sizes):
        at = [sum(sizes[:i]) for i in range(len(sizes))]
        return [range(start, start + size) for start, size in zip(at, sizes)], [
            pltpu.make_async_copy(
                source.at[pl.ds(start, size)], target.at[pl.ds(start, size)], sems.at[i]
            )
            for i, (start, size) in enumerate(zip(at, sizes))
        ]

    kparts, kcopies = copies(k_hbm, kbuf, ksem, KEY_PARTS)
    vparts, vcopies = copies(v_hbm, vbuf, vsem, VALUE_PARTS)
    for copy in small + kcopies:
        copy.start(priority=0)
    for copy in vcopies:
        copy.start(priority=1)
    m_ref[...] = jnp.full(m_ref.shape, FLOOR, jnp.float32)
    l_ref[...] = jnp.zeros_like(l_ref)
    acc_ref[...] = jnp.zeros_like(acc_ref)
    for copy in small:
        copy.wait()

    def place(c):
        span = map_ref[c]
        row = lax.shift_right_logical(span, CPR.bit_length() - 1)
        return row, lax.bitwise_and(span, CPR - 1) * SPAN < len_ref[row]

    def folded(x, op):
        tiles = [x[:, i * LANES : (i + 1) * LANES] for i in range(SPAN // LANES)]
        return op(op(tiles[0], tiles[1]), op(tiles[2], tiles[3]))

    for part, copy in zip(kparts, kcopies):
        copy.wait()
        for c in part:
            row, live = place(c)
            s = lax.dot_general(
                q_ref[row], kbuf[c], (((1,), (1,)), ((), ())), preferred_element_type=jnp.float32
            )
            s_ref[c] = s
            m_ref[row] = jnp.maximum(
                m_ref[row], jnp.where(live, folded(s, jnp.maximum), FLOOR)
            )
    m_ref[...] = jnp.broadcast_to(jnp.max(m_ref[...], axis=2, keepdims=True), m_ref.shape)

    for part, copy in zip(vparts, vcopies):
        copy.wait()
        for c in part:
            row, live = place(c)
            top = jnp.where(live, m_ref[row], -FLOOR)
            top = jnp.concatenate([top] * (SPAN // LANES), axis=1)
            p = jnp.exp2((s_ref[c] - top) * (SCALE * LOG2E)).astype(jnp.bfloat16)
            l_ref[row] += folded(p.astype(jnp.float32), jnp.add)
            acc_ref[row] += jnp.dot(p, vbuf[c], preferred_element_type=jnp.float32)

    l = jnp.broadcast_to(jnp.sum(l_ref[...], axis=2, keepdims=True), l_ref.shape)
    some = l > 0.0
    safe = jnp.where(some, l, 1.0)
    lse = jnp.where(some, m_ref[...] * SCALE + jnp.log(safe), NOTHING)
    out = acc_ref[...] / safe
    power = power_of(out)
    out = coded(out, power)
    flat = out_ref.reshape(out_ref.shape[0], PAY, HD)
    for c in range(2):
        for i, values in enumerate((out, lse, jnp.broadcast_to(power, out.shape))):
            for r in range(ROWS):
                order[c, i, pl.ds(r, HALF, stride=ROWS), :] = values[r, c * HALF : (c + 1) * HALF]
        payload = jnp.concatenate([order[c, 0], header(order[c, 1], order[c, 2])], axis=0)
        payload = fixed(payload)
        for z in range(out_ref.shape[0] // 2):
            flat[2 * z + c] = payload


def merge_kernel(in_ref, out_ref):
    flat = in_ref.reshape(in_ref.shape[0], PAY, HD)
    halves = [range(0, 8), range(8, 16)]
    heads = [read_headers(flat, half) for half in halves]
    peak = jnp.max(jnp.maximum(heads[0][0], heads[1][0]), axis=0, keepdims=True)
    weights = [jnp.exp(lse - peak) for lse, _ in heads]
    mass = jnp.sum(weights[0] + weights[1], axis=0, keepdims=True)
    lse = peak + jnp.log(mass)
    weights = [w * scale / mass for w, (_, scale) in zip(weights, heads)]
    groups = BLOCKS
    rows = by_block([t for w in weights for t in (w, pltpu.roll(w, 4, 0))])
    parts = [
        weighted_sum(flat, rows[g : g + 1], [k * groups + g for k in range(BLOCKS)])
        for g in range(groups)
    ]
    out = (parts[0] + parts[1]) + (parts[2] + parts[3])
    power = power_of(out)
    payload = fixed(jnp.concatenate([coded(out, power), header(lse, power)], axis=0))
    sent = out_ref.reshape(out_ref.shape[0], PAY, HD)
    for i in range(out_ref.shape[0]):
        sent[i] = payload


def gather_kernel(in_ref, out_ref):
    flat = in_ref.reshape(in_ref.shape[0], PAY, HD)
    groups = in_ref.shape[0] // BLOCKS
    heads = [read_headers(flat, range(8 * t, 8 * t + 8)) for t in range(2)]
    peak = jnp.maximum(heads[0][0], heads[1][0])
    peak = jnp.maximum(peak, pltpu.roll(peak, 4, 0))
    weights = [jnp.exp(lse - peak) for lse, _ in heads]
    mass = weights[0] + weights[1]
    mass = mass + pltpu.roll(mass, 4, 0)
    weights = [w * scale / mass for w, (_, scale) in zip(weights, heads)]
    rows = by_block([t for w in weights for t in (w, pltpu.roll(w, 4, 0))])
    for g in range(groups):
        out_ref[g * PAIRS : (g + 1) * PAIRS] = weighted_sum(
            flat, rows[g : g + 1], [groups * k + g for k in range(BLOCKS)]
        )
    out_ref[groups * PAIRS : groups * PAIRS + 8] = peak + jnp.log(mass)


def half_product(ref, w_ref, c):
    groups = ref.shape[0] // PAIRS
    half = ref[...]
    wide = HALF * HD
    heads = [
        half[x * PAIRS + ROWS * h : x * PAIRS + ROWS * (h + 1)]
        for x in range(groups)
        for h in range(HALF)
    ]
    columns = [
        w_ref[:, pl.ds(pl.multiple_of((x * 2 + c) * wide, wide), wide)] for x in range(groups)
    ]
    return lax.dot_general(
        jnp.concatenate(heads, axis=1).astype(jnp.bfloat16),
        jnp.concatenate(columns, axis=1),
        (((1,), (1,)), ((), ())),
        preferred_element_type=jnp.float32,
    )


def own_kernel(mine_ref, w_ref, out_ref):
    out_ref[...] = half_product(mine_ref, w_ref, lax.axis_index("core"))


def project_kernel(mine_ref, other_ref, own_ref, w_ref, proj_ref, mass_ref):
    groups = mine_ref.shape[0] // PAIRS
    core = lax.axis_index("core")
    proj_ref[...] = own_ref[...] + half_product(other_ref, w_ref, 1 - core)
    tail = slice(groups * PAIRS, groups * PAIRS + 8)
    mine, other = mine_ref[tail], other_ref[tail]
    halves = [jnp.where(core == 0, mine, other), jnp.where(core == 0, other, mine)]
    pair, lane = iota((PAIRS, LANES), 0), iota((PAIRS, LANES), 1)
    table = jnp.zeros((PAIRS, LANES), jnp.float32)
    for c in range(2):
        lse = halves[c]
        own = jnp.where(iota(lse.shape, 0) == lax.axis_index("x"), lse, 0.0)
        own = jnp.sum(own, axis=0, keepdims=True)
        column = jnp.sum(jnp.where(lane == pair, own, 0.0), axis=1, keepdims=True)
        table = jnp.where(lane == c * HALF + pair // ROWS, column, table)
    table = sum(table[8 * i : 8 * (i + 1)] for i in range(PAIRS // 8))
    mass_ref[...] = (table[:ROWS] + table[ROWS:])[:, :GROUP]


def shards(queries, keys, values, lengths, span_map, w_out):
    slots = span_map.shape[0]
    z, y, x = lax.axis_size("z"), lax.axis_size("y"), lax.axis_size("x")
    f32, bf16 = jnp.float32, jnp.bfloat16
    cache = (slots, SPAN, HD)
    inputs = (queries, lengths, span_map, keys.reshape(cache), values.reshape(cache))
    inputs = [pltpu.with_memory_space_constraint(x, pltpu.HBM) for x in inputs]
    part = pl.pallas_call(
        attend_kernel,
        out_shape=pltpu.VMEM((z * 2, PAY // 2, 2, HD), jnp.int16),
        in_specs=[HBM] * 5,
        out_specs=VMEM,
        scratch_shapes=[
            pltpu.VMEM((ROWS, GROUP, HD), bf16),
            pltpu.SMEM((ROWS,), jnp.int32),
            pltpu.SMEM((slots,), jnp.int32),
            pltpu.VMEM(cache, bf16),
            pltpu.VMEM(cache, bf16),
            pltpu.VMEM((slots, GROUP, SPAN), f32),
            pltpu.VMEM((ROWS, GROUP, LANES), f32),
            pltpu.VMEM((ROWS, GROUP, LANES), f32),
            pltpu.VMEM((ROWS, GROUP, HD), f32),
            pltpu.VMEM((2, 3, PAIRS, LANES), f32),
            pltpu.SemaphoreType.DMA((3,)),
            pltpu.SemaphoreType.DMA((len(KEY_PARTS),)),
            pltpu.SemaphoreType.DMA((len(VALUE_PARTS),)),
        ],
        compiler_params=pltpu.CompilerParams(vmem_limit_bytes=24 * 2**20),
        name="attend",
    )(*inputs)
    part = lax.all_to_all(part, ("z", "core"), 0, 0, tiled=True)
    part = pl.pallas_call(
        merge_kernel,
        out_shape=jax.ShapeDtypeStruct((y * x, PAY // 2, 2, HD), jnp.int16),
        in_specs=[VMEM],
        out_specs=VMEM,
        compiler_params=pltpu.CompilerParams(vmem_limit_bytes=8 * 2**20),
        name="merge",
    )(part)
    part = lax.all_to_all(part, ("y", "x"), 0, 0, tiled=True)
    mine = pl.pallas_call(
        gather_kernel,
        out_shape=pltpu.VMEM((x * PAIRS + 8, HD), f32),
        in_specs=[VMEM],
        out_specs=VMEM,
        compiler_params=pltpu.CompilerParams(vmem_limit_bytes=8 * 2**20),
        name="gather",
    )(part)
    other = lax.ppermute(mine, "core", [(0, 1), (1, 0)])
    own = pl.pallas_call(
        own_kernel,
        out_shape=pltpu.VMEM((ROWS, w_out.shape[1]), f32),
        in_specs=[VMEM, VMEM],
        out_specs=VMEM,
        compiler_params=pltpu.CompilerParams(vmem_limit_bytes=8 * 2**20),
        cost_estimate=pl.CostEstimate(
            flops=ROWS * w_out.size, bytes_accessed=w_out.size, transcendentals=0
        ),
        name="own",
    )(mine, w_out.T)
    return pl.pallas_call(
        project_kernel,
        out_shape=(
            jax.ShapeDtypeStruct((ROWS, w_out.shape[1]), f32),
            jax.ShapeDtypeStruct((ROWS, GROUP), f32),
        ),
        in_specs=[VMEM] * 4,
        out_specs=(VMEM, VMEM),
        compiler_params=pltpu.CompilerParams(vmem_limit_bytes=8 * 2**20),
        name="project",
    )(mine, other, own, w_out.T)


def solution(mesh):
    fine = Mesh(mesh.devices.reshape(8, 4, 2, 4), ("z", "y", "core", "x"))
    ctx = ("z", "y", "core")
    placed = (
        P(None, "x", None),
        P(ctx, "x", None, None),
        P(ctx, "x", None, None),
        P(),
        P(ctx),
        P(None, ctx),
    )
    return jax.shard_map(
        shards,
        mesh=fine,
        in_specs=placed,
        out_specs=(P(None, ctx), P(None, "x")),
        check_vma=False,
    )
```

```python
import functools
import math

import jax
import jax.numpy as jnp
from jax import lax
from jax.experimental import pallas as pl
from jax.experimental.pallas import tpu as pltpu
from jax.sharding import Mesh, PartitionSpec as P

ROWS, HD, GROUP, SPAN, CPR = 4, 128, 16, 512, 512
HALF = GROUP // 2
PAIRS = ROWS * HALF
PAY = PAIRS + 2
LANES = 128
BLOCKS = LANES // PAIRS
FLOOR = -1e30
NOTHING = -32000.0
TINY = 2.0**-110
STEPS = 32760.0
SCALE = 1.0 / math.sqrt(HD)
LOG2E = math.log2(math.e)
KEY_PARTS = (16, 16)
VALUE_PARTS = (16, 16)

VMEM = pl.BlockSpec(memory_space=pltpu.VMEM)
HBM = pl.BlockSpec(memory_space=pltpu.HBM)


def iota(shape, axis):
    return lax.broadcasted_iota(jnp.int32, shape, axis)


def fixed(x):
    return x.astype(jnp.int32).astype(jnp.int16)


def header(lse, power):
    whole = jnp.floor(lse)
    rest = (lse - whole) * 32768.0
    first = jnp.minimum(jnp.floor(rest), 32767.0)
    second = jnp.minimum(jnp.floor((rest - first) * 32768.0), 32767.0)
    shape = (PAIRS, LANES)
    block = iota(shape, 1) // PAIRS
    kind = jnp.where(block == 0, whole, jnp.where(block == 1, first, second))
    kind = jnp.where(block == 3, power, kind)
    row = jnp.sum(
        jnp.where(iota(shape, 1) % PAIRS == iota(shape, 0), kind, 0.0), axis=0, keepdims=True
    )
    return jnp.broadcast_to(row, (2, LANES))


def read_headers(flat, members):
    rows = [flat[i, PAIRS:PAY].astype(jnp.int32).astype(jnp.float32)[0:1] for i in members]
    rows = jnp.concatenate(rows, axis=0)
    block = iota(rows.shape, 1) // PAIRS
    unit = jnp.where(block == 0, 1.0, jnp.where(block == 1, 2.0**-15, 2.0**-30))
    lse = over_blocks(jnp.where(block == 3, 0.0, rows * unit), jnp.add)
    scale = over_blocks(jnp.where(block == 3, rows, 0.0), jnp.add)
    return lse, jnp.exp2(scale * (1.0 / 256.0)) * (1.0 / STEPS)


def by_block(tiles):
    block = iota(tiles[0].shape, 1) // PAIRS
    out = tiles[0]
    for k in range(1, BLOCKS):
        out = jnp.where(block == k, tiles[k], out)
    return out


def power_of(out):
    largest = jnp.max(jnp.abs(out), axis=-1, keepdims=True)
    return jnp.ceil(jnp.log2(jnp.maximum(largest, TINY)) * 256.0 + 1.0)


def coded(out, power):
    return jnp.round(out * (jnp.exp2(power * (-1.0 / 256.0)) * STEPS))


def weighted_sum(flat, row, members):
    shape = (PAIRS, LANES)
    block = iota(shape, 1) // PAIRS
    spread = jnp.where(iota(shape, 1) % PAIRS == iota(shape, 0), row, 0.0)
    terms = []
    for k, i in enumerate(members):
        column = jnp.sum(jnp.where(block == k, spread, 0.0), axis=1, keepdims=True)
        terms.append(column * flat[i, 0:PAIRS].astype(jnp.int32).astype(jnp.float32))
    return (terms[0] + terms[1]) + (terms[2] + terms[3])


def over_blocks(x, op):
    step = PAIRS
    while step < LANES:
        x = op(x, pltpu.roll(x, step, 1))
        step *= 2
    return x


def attend_kernel(
    q_hbm, len_hbm, map_hbm, k_hbm, v_hbm, out_ref,
    q_ref, len_ref, map_ref, kbuf, vbuf, s_ref, m_ref, l_ref, acc_ref, order, sem, ksem, vsem,
):
    small = [
        pltpu.make_async_copy(source, target, sem.at[i])
        for i, (source, target) in enumerate(
            [(map_hbm, map_ref), (len_hbm, len_ref), (q_hbm, q_ref)]
        )
    ]

    def copies(source, target, sems, sizes):
        at = [sum(sizes[:i]) for i in range(len(sizes))]
        return [range(start, start + size) for start, size in zip(at, sizes)], [
            pltpu.make_async_copy(
                source.at[pl.ds(start, size)], target.at[pl.ds(start, size)], sems.at[i]
            )
            for i, (start, size) in enumerate(zip(at, sizes))
        ]

    kparts, kcopies = copies(k_hbm, kbuf, ksem, KEY_PARTS)
    vparts, vcopies = copies(v_hbm, vbuf, vsem, VALUE_PARTS)
    for copy in small + kcopies:
        copy.start(priority=0)
    for copy in vcopies:
        copy.start(priority=1)
    m_ref[...] = jnp.full(m_ref.shape, FLOOR, jnp.float32)
    l_ref[...] = jnp.zeros_like(l_ref)
    acc_ref[...] = jnp.zeros_like(acc_ref)
    for copy in small:
        copy.wait()

    def place(c):
        span = map_ref[c]
        row = lax.shift_right_logical(span, CPR.bit_length() - 1)
        return row, lax.bitwise_and(span, CPR - 1) * SPAN < len_ref[row]

    def folded(x, op):
        tiles = [x[:, i * LANES : (i + 1) * LANES] for i in range(SPAN // LANES)]
        return op(op(tiles[0], tiles[1]), op(tiles[2], tiles[3]))

    for part, copy in zip(kparts, kcopies):
        copy.wait()
        for c in part:
            row, live = place(c)
            s = lax.dot_general(
                q_ref[row], kbuf[c], (((1,), (1,)), ((), ())), preferred_element_type=jnp.float32
            )
            s_ref[c] = s
            m_ref[row] = jnp.maximum(
                m_ref[row], jnp.where(live, folded(s, jnp.maximum), FLOOR)
            )
    m_ref[...] = jnp.broadcast_to(jnp.max(m_ref[...], axis=2, keepdims=True), m_ref.shape)

    for part, copy in zip(vparts, vcopies):
        copy.wait()
        for c in part:
            row, live = place(c)
            top = jnp.where(live, m_ref[row], -FLOOR)
            top = jnp.concatenate([top] * (SPAN // LANES), axis=1)
            p = jnp.exp2((s_ref[c] - top) * (SCALE * LOG2E)).astype(jnp.bfloat16)
            l_ref[row] += folded(p.astype(jnp.float32), jnp.add)
            acc_ref[row] += jnp.dot(p, vbuf[c], preferred_element_type=jnp.float32)

    l = jnp.broadcast_to(jnp.sum(l_ref[...], axis=2, keepdims=True), l_ref.shape)
    some = l > 0.0
    safe = jnp.where(some, l, 1.0)
    lse = jnp.where(some, m_ref[...] * SCALE + jnp.log(safe), NOTHING)
    out = acc_ref[...] / safe
    power = power_of(out)
    out = coded(out, power)
    flat = out_ref.reshape(out_ref.shape[0], PAY, HD)
    for c in range(2):
        for i, values in enumerate((out, lse, jnp.broadcast_to(power, out.shape))):
            for r in range(ROWS):
                order[c, i, pl.ds(r, HALF, stride=ROWS), :] = values[r, c * HALF : (c + 1) * HALF]
        payload = jnp.concatenate([order[c, 0], header(order[c, 1], order[c, 2])], axis=0)
        payload = fixed(payload)
        for z in range(out_ref.shape[0] // 2):
            flat[2 * z + c] = payload


def merge_kernel(in_ref, out_ref):
    flat = in_ref.reshape(in_ref.shape[0], PAY, HD)
    halves = [range(0, 8), range(8, 16)]
    heads = [read_headers(flat, half) for half in halves]
    peak = jnp.max(jnp.maximum(heads[0][0], heads[1][0]), axis=0, keepdims=True)
    weights = [jnp.exp(lse - peak) for lse, _ in heads]
    mass = jnp.sum(weights[0] + weights[1], axis=0, keepdims=True)
    lse = peak + jnp.log(mass)
    weights = [w * scale / mass for w, (_, scale) in zip(weights, heads)]
    groups = BLOCKS
    rows = by_block([t for w in weights for t in (w, pltpu.roll(w, 4, 0))])
    parts = [
        weighted_sum(flat, rows[g : g + 1], [k * groups + g for k in range(BLOCKS)])
        for g in range(groups)
    ]
    out = (parts[0] + parts[1]) + (parts[2] + parts[3])
    power = power_of(out)
    payload = fixed(jnp.concatenate([coded(out, power), header(lse, power)], axis=0))
    sent = out_ref.reshape(out_ref.shape[0], PAY, HD)
    for i in range(out_ref.shape[0]):
        sent[i] = payload


def gather_kernel(in_ref, out_ref):
    flat = in_ref.reshape(in_ref.shape[0], PAY, HD)
    groups = in_ref.shape[0] // BLOCKS
    heads = [read_headers(flat, range(8 * t, 8 * t + 8)) for t in range(2)]
    peak = jnp.maximum(heads[0][0], heads[1][0])
    peak = jnp.maximum(peak, pltpu.roll(peak, 4, 0))
    weights = [jnp.exp(lse - peak) for lse, _ in heads]
    mass = weights[0] + weights[1]
    mass = mass + pltpu.roll(mass, 4, 0)
    weights = [w * scale / mass for w, (_, scale) in zip(weights, heads)]
    rows = by_block([t for w in weights for t in (w, pltpu.roll(w, 4, 0))])
    for g in range(groups):
        out_ref[g * PAIRS : (g + 1) * PAIRS] = weighted_sum(
            flat, rows[g : g + 1], [groups * k + g for k in range(BLOCKS)]
        )
    out_ref[groups * PAIRS : groups * PAIRS + 8] = peak + jnp.log(mass)


def half_product(ref, w_ref, c):
    groups = ref.shape[0] // PAIRS
    half = ref[...]
    wide = HALF * HD
    heads = [
        half[x * PAIRS + ROWS * h : x * PAIRS + ROWS * (h + 1)]
        for x in range(groups)
        for h in range(HALF)
    ]
    columns = [
        w_ref[:, pl.ds(pl.multiple_of((x * 2 + c) * wide, wide), wide)] for x in range(groups)
    ]
    return lax.dot_general(
        jnp.concatenate(heads, axis=1).astype(jnp.bfloat16),
        jnp.concatenate(columns, axis=1),
        (((1,), (1,)), ((), ())),
        preferred_element_type=jnp.float32,
    )


def mass_rows(ref, c):
    tile = ref[ref.shape[0] - 8 : ref.shape[0]]
    own = jnp.where(iota(tile.shape, 0) == lax.axis_index("x"), tile, 0.0)
    own = jnp.sum(own, axis=0, keepdims=True)
    pair, lane = iota((PAIRS, LANES), 0), iota((PAIRS, LANES), 1)
    column = jnp.sum(jnp.where(lane == pair, own, 0.0), axis=1, keepdims=True)
    table = jnp.where(lane == c * HALF + pair // ROWS, column, 0.0)
    table = sum(table[8 * i : 8 * (i + 1)] for i in range(PAIRS // 8))
    return (table[:ROWS] + table[ROWS:])[:, :GROUP]


def own_kernel(mine_ref, w_ref, out_ref, mass_ref):
    core = lax.axis_index("core")
    out_ref[...] = half_product(mine_ref, w_ref, core)
    mass_ref[...] = mass_rows(mine_ref, core)


def project_kernel(other_ref, own_ref, own_mass_ref, w_ref, proj_ref, mass_ref):
    other = 1 - lax.axis_index("core")
    proj_ref[...] = own_ref[...] + half_product(other_ref, w_ref, other)
    mass_ref[...] = own_mass_ref[...] + mass_rows(other_ref, other)


def shards(queries, keys, values, lengths, span_map, w_out):
    slots = span_map.shape[0]
    z, y, x = lax.axis_size("z"), lax.axis_size("y"), lax.axis_size("x")
    f32, bf16 = jnp.float32, jnp.bfloat16
    cache = (slots, SPAN, HD)
    inputs = (queries, lengths, span_map, keys.reshape(cache), values.reshape(cache))
    inputs = [pltpu.with_memory_space_constraint(x, pltpu.HBM) for x in inputs]
    part = pl.pallas_call(
        attend_kernel,
        out_shape=pltpu.VMEM((z * 2, PAY // 2, 2, HD), jnp.int16),
        in_specs=[HBM] * 5,
        out_specs=VMEM,
        scratch_shapes=[
            pltpu.VMEM((ROWS, GROUP, HD), bf16),
            pltpu.SMEM((ROWS,), jnp.int32),
            pltpu.SMEM((slots,), jnp.int32),
            pltpu.VMEM(cache, bf16),
            pltpu.VMEM(cache, bf16),
            pltpu.VMEM((slots, GROUP, SPAN), f32),
            pltpu.VMEM((ROWS, GROUP, LANES), f32),
            pltpu.VMEM((ROWS, GROUP, LANES), f32),
            pltpu.VMEM((ROWS, GROUP, HD), f32),
            pltpu.VMEM((2, 3, PAIRS, LANES), f32),
            pltpu.SemaphoreType.DMA((3,)),
            pltpu.SemaphoreType.DMA((len(KEY_PARTS),)),
            pltpu.SemaphoreType.DMA((len(VALUE_PARTS),)),
        ],
        compiler_params=pltpu.CompilerParams(vmem_limit_bytes=24 * 2**20),
        name="attend",
    )(*inputs)
    part = lax.all_to_all(part, ("z", "core"), 0, 0, tiled=True)
    part = pl.pallas_call(
        merge_kernel,
        out_shape=jax.ShapeDtypeStruct((y * x, PAY // 2, 2, HD), jnp.int16),
        in_specs=[VMEM],
        out_specs=VMEM,
        compiler_params=pltpu.CompilerParams(vmem_limit_bytes=8 * 2**20),
        name="merge",
    )(part)
    part = lax.all_to_all(part, ("y", "x"), 0, 0, tiled=True)
    mine = pl.pallas_call(
        gather_kernel,
        out_shape=pltpu.VMEM((x * PAIRS + 8, HD), f32),
        in_specs=[VMEM],
        out_specs=VMEM,
        compiler_params=pltpu.CompilerParams(vmem_limit_bytes=8 * 2**20),
        name="gather",
    )(part)
    other = lax.ppermute(mine, "core", [(0, 1), (1, 0)])
    own, own_mass = pl.pallas_call(
        own_kernel,
        out_shape=(
            pltpu.VMEM((ROWS, w_out.shape[1]), f32),
            pltpu.VMEM((ROWS, GROUP), f32),
        ),
        in_specs=[VMEM, VMEM],
        out_specs=(VMEM, VMEM),
        compiler_params=pltpu.CompilerParams(vmem_limit_bytes=8 * 2**20),
        cost_estimate=pl.CostEstimate(
            flops=ROWS * w_out.size, bytes_accessed=w_out.size, transcendentals=0
        ),
        name="own",
    )(mine, w_out.T)
    return pl.pallas_call(
        project_kernel,
        out_shape=(
            jax.ShapeDtypeStruct((ROWS, w_out.shape[1]), f32),
            jax.ShapeDtypeStruct((ROWS, GROUP), f32),
        ),
        in_specs=[VMEM] * 4,
        out_specs=(VMEM, VMEM),
        compiler_params=pltpu.CompilerParams(vmem_limit_bytes=8 * 2**20),
        name="project",
    )(other, own, own_mass, w_out.T)


def solution(mesh):
    fine = Mesh(mesh.devices.reshape(8, 4, 2, 4), ("z", "y", "core", "x"))
    ctx = ("z", "y", "core")
    placed = (
        P(None, "x", None),
        P(ctx, "x", None, None),
        P(ctx, "x", None, None),
        P(),
        P(ctx),
        P(None, ctx),
    )
    return jax.shard_map(
        shards,
        mesh=fine,
        in_specs=placed,
        out_specs=(P(None, ctx), P(None, "x")),
        check_vma=False,
    )
```
